256 devices in a mesh: dp: 8 (over y, core), expert: 32 (over x, z).
Axes of the slice: x: 4, y: 4, z: 8, core: 2. Of those that a mesh axis runs over, the one named last changes fastest.
Arguments:
- tokens: bfloat16 [8192, 2048], P(('dp', 'expert')), may hold values from -6 to 6
- expert_ids: int32 [8192, 8], P(('dp', 'expert')), may hold values from 0 to 31, all different within a row; in each aligned block of 32 rows (0 to 31, 32 to 63, ...) at most 12 rows name the same one
- gate_weights: float32 [8192, 8], P(('dp', 'expert')), may hold values from 0.05 to 0.5
- cotangent: bfloat16 [8192, 2048], P(('dp', 'expert')), may hold values from -6 to 6
- w_gate: bfloat16 [32, 1536, 2048], P('expert', 'dp'), may hold values from -0.125 to 0.125
- w_up: bfloat16 [32, 1536, 2048], P('expert', 'dp'), may hold values from -0.125 to 0.125
- w_down: bfloat16 [32, 1536, 2048], P('expert', 'dp'), may hold values from -0.15625 to 0.15625
Outputs:
- layer_out: bfloat16 [8192, 2048], P(('dp', 'expert'))
- input_grad: bfloat16 [8192, 2048], P(('dp', 'expert'))
The draws below stay inside these ranges and needn't reach their ends.
Inputs may be any that keep to these rules, and one draw needn't show every extreme that they name: `expert_ids`: each row names 8 different experts. Among the 32 rows of one device (aligned blocks of rows), no expert is named by more than 12 rows, and in every draw some expert is named by exactly 12 rows of some device.
All inputs are finite; a program needn't handle non-finite values.
Results may differ from the reference program's by a relative error of at most 0.011.
Values may be sent and summed in bfloat16 or wider, within the bound.
A program may use at most 128 MiB of HBM per device.

```python
import math
import jax
import jax.numpy as jnp
import numpy as np
from jax import lax

D = 2048
HID = 1536
EXPERTS = 32
TOPK = 8
TOK_DEV = 32
TOKENS = 8192
CAP = 12


def level_of(rng, dims, pieces, low, high):
    def one(axis_at, blocks):
        draws = jax.random.uniform(jax.random.fold_in(jax.random.fold_in(rng, 6), axis_at), (blocks,), jnp.float32, low / len(pieces), high / len(pieces))
        return jnp.repeat(jnp.exp(draws), dims[axis_at] // blocks).reshape((-1,) + (1,) * (len(dims) - axis_at - 1))

    level = one(*pieces[0])
    for cut in pieces[1:]:
        level = level * one(*cut)
    return level


def shared_out(key, own, number, rows, count, top, bound, slope):
    ranking = jax.random.permutation(key, count)
    crowded, ordinary = portions_of(count, rows * top, bound, slope, True), portions_of(count, rows * top, bound, slope, False)
    places = jnp.arange(count)

    def named(tallies, turn):
        used = int((tallies > 0).sum())
        fixed = max(1, used // 4)
        passed = fixed + (places - fixed + turn * (used - fixed)) % max(1, count - fixed)
        return jnp.zeros((count,), jnp.int32).at[ranking[jnp.where(places < fixed, places, passed)]].set(jnp.asarray(tallies, jnp.int32))

    tallies = jnp.where(number % 4 == 0, named(crowded, number // 4), named(ordinary, number - number // 4 - 1))
    mixed = jax.random.permutation(jax.random.fold_in(own, 3), count)
    donor, taker = mixed[0:count // 2 * 2:2], mixed[1:count // 2 * 2:2]
    room = jnp.minimum(tallies[donor] - 1, bound - tallies[taker]) // 2
    room = jnp.where((donor == ranking[0]) | (taker == ranking[0]) | (tallies[taker] == 0), 0, jnp.maximum(room, 0))
    passed = jax.random.randint(jax.random.fold_in(own, 4), (count // 2,), 0, 1 << 20) % (room + 1)
    tallies = tallies.at[donor].add(-passed).at[taker].add(passed)
    members = jnp.searchsorted(jnp.cumsum(tallies), jnp.arange(rows * top), side="right").astype(jnp.int32)
    table = members.reshape(top, rows).T
    table = table[jax.random.permutation(jax.random.fold_in(own, 1), rows)]
    turn = jax.random.randint(jax.random.fold_in(own, 2), (rows, 1), 0, top)
    return jnp.take_along_axis(table, (jnp.arange(top)[None, :] + turn) % top, axis=1)


def portions_of(number_of, total, reach, lean, full):
    weights = [(1 << 20) // math.isqrt(standing ** lean) + 1 for standing in range(1, number_of + 1)]
    largest = reach if full else min(reach, max(-(-total // number_of), total * weights[0] // sum(weights)))
    least = 1 if total - largest >= number_of - 1 else 0
    given, rest = [largest] + [least] * (number_of - 1), total - largest - least * (number_of - 1)
    while rest > 0:
        candidates = [i for i in range(1, number_of) if given[i] < largest] or [i for i in range(1, number_of) if given[i] < reach]
        whole, left = sum([weights[i] for i in candidates]), rest
        for i in candidates:
            extra = min(reach - given[i], max(1, left * weights[i] // whole), rest)
            given[i] = given[i] + extra
            rest = rest - extra
    return np.array(given)


def normal_values(own_key, dims, width, bound, pieces=(), kind=jnp.bfloat16):
    entries = jax.random.normal(own_key, dims, jnp.float32) * width
    if len(pieces) > 0:
        entries = level_of(own_key, dims, pieces, -0.22, 0.18) * entries
    return jnp.clip(entries, min=-bound, max=bound).astype(kind)


def setup_inputs(seed: int = 0) -> dict:
    splits = jax.random.split(jax.random.key(seed), 8)
    tokens = normal_values(splits[0], (TOKENS, D), 1.0, 6.0, ((0, 256),))
    expert_ids_keys = jax.random.split(jax.random.fold_in(splits[1], 1), TOKENS // TOK_DEV)
    expert_ids_turns = jax.random.permutation(jax.random.fold_in(splits[1], 3), TOKENS // TOK_DEV)
    expert_ids = jax.vmap(lambda own, number: shared_out(jax.random.fold_in(splits[1], 2), own, number, TOK_DEV, EXPERTS, TOPK, CAP, 2))(expert_ids_keys, expert_ids_turns).reshape((TOKENS, TOPK))
    gate_weights = jnp.clip(jnp.exp(math.log(0.5) - 2.3025851 * jax.random.uniform(splits[2], (TOKENS, TOPK), jnp.float32) ** level_of(splits[2], (TOKENS, TOPK), ((0, 256),), -0.2, 0.2)), 0.05, 0.5)
    cotangent = normal_values(splits[3], (TOKENS, D), 1.0, 6.0, ((0, 256),))
    w_gate = normal_values(splits[4], (EXPERTS, HID, D), D ** -0.5, 0.125, ((0, 32), (1, 8)))
    w_up = normal_values(splits[5], (EXPERTS, HID, D), D ** -0.5, 0.125, ((0, 32), (1, 8)))
    w_down = normal_values(splits[6], (EXPERTS, HID, D), HID ** -0.5, 0.15625, ((0, 32), (1, 8)))
    return {"tokens": tokens, "expert_ids": expert_ids, "gate_weights": gate_weights, "cotangent": cotangent, "w_gate": w_gate, "w_up": w_up, "w_down": w_down}


def one_expert(rows_in, rows_back, gate_mat, up_mat, down_mat):
    pre_gate = jnp.dot(rows_in, gate_mat.T, preferred_element_type=jnp.float32)
    pre_up = jnp.dot(rows_in, up_mat.T, preferred_element_type=jnp.float32)
    sig_gate = jax.nn.sigmoid(pre_gate)
    silu_gate = pre_gate * sig_gate
    hidden = (silu_gate * pre_up).astype(jnp.bfloat16)
    expert_out = jnp.dot(hidden, down_mat, preferred_element_type=jnp.float32)
    back_term = jnp.dot(rows_back, down_mat.T, preferred_element_type=jnp.float32)
    grad_gate = (back_term * pre_up * sig_gate * (1.0 + pre_gate * (1.0 - sig_gate))).astype(jnp.bfloat16)
    grad_up = (back_term * silu_gate).astype(jnp.bfloat16)
    slot_grad = jnp.dot(grad_gate, gate_mat, preferred_element_type=jnp.float32)
    slot_grad = slot_grad + jnp.dot(grad_up, up_mat, preferred_element_type=jnp.float32)
    return expert_out.astype(jnp.bfloat16), slot_grad.astype(jnp.bfloat16)


def reference(tokens, expert_ids, gate_weights, cotangent, w_gate, w_up, w_down):
    blocks = TOKENS // TOK_DEV
    flat_ids = expert_ids.reshape(blocks, TOK_DEV * TOPK)
    onehot = (flat_ids[:, :, None] == jnp.arange(EXPERTS, dtype=jnp.int32)[None, None, :]).astype(jnp.int32)
    slot_rank = jnp.sum((jnp.cumsum(onehot, axis=1) - onehot) * onehot, axis=2)
    block_id = jnp.arange(blocks, dtype=jnp.int32)[:, None]
    slot_index = ((flat_ids * blocks + block_id) * CAP + slot_rank).reshape(-1).astype(jnp.int32)
    token_of = jnp.arange(TOKENS * TOPK, dtype=jnp.int32) // TOPK
    slot_owner = jnp.full((EXPERTS * blocks * CAP,), TOKENS, jnp.int32).at[slot_index].set(token_of)
    padded_in = jnp.concatenate([tokens, jnp.zeros((1, D), tokens.dtype)], axis=0)
    padded_back = jnp.concatenate([cotangent, jnp.zeros((1, D), cotangent.dtype)], axis=0)

    def run_expert(bundle):
        row_index, gate_mat, up_mat, down_mat = bundle
        return one_expert(padded_in[row_index], padded_back[row_index], gate_mat, up_mat, down_mat)

    outs, grads = lax.map(run_expert, (slot_owner.reshape(EXPERTS, blocks * CAP), w_gate, w_up, w_down))
    picked_out = outs.reshape(-1, D)[slot_index].reshape(TOKENS, TOPK, D).astype(jnp.float32)
    picked_grad = grads.reshape(-1, D)[slot_index].reshape(TOKENS, TOPK, D).astype(jnp.float32)
    layer_out = jnp.einsum('tk,tkd->td', gate_weights, picked_out)
    input_grad = jnp.einsum('tk,tkd->td', gate_weights, picked_grad)
    return layer_out.astype(jnp.bfloat16), input_grad.astype(jnp.bfloat16)
```

```python
import functools

import jax
import jax.numpy as jnp
from jax import lax
from jax.experimental import pallas as pl
from jax.experimental.pallas import tpu as pltpu
from jax.sharding import PartitionSpec as P

MESH = pl.DeviceIdType.MESH
NX, NY, NZ = 4, 4, 8
CAP = 12
CHUNKS = 4
NT = (((1,), (1,)), ((), ()))
BF = jnp.bfloat16
F32 = jnp.float32


def mm(a, b):
    return jnp.dot(a, b, preferred_element_type=F32)


def mm_nt(a, b):
    return lax.dot_general(a, b, NT, preferred_element_type=F32)


def kernel(
    tok_ref, cot_ref, meta_ref, wg_ref, wu_ref, wd_ref, out_a, out_b,
    w, t, meta, sel, comb, xs, rows, hid, acc, ys, yr, part, rsend, rrecv,
    ssem, rsem, lsem,
):
    dp, ex = lax.axis_index("dp"), lax.axis_index("expert")
    y, c = dp // 2, lax.rem(dp, 2)
    x, z = ex // NZ, lax.rem(ex, NZ)
    tok_rows, width = tok_ref.shape
    unit = wg_ref.shape[0]
    half = unit // 2
    seg = NZ * CAP
    cw = width // CHUNKS

    def at_y(step):
        return {"dp": lax.rem(y + step + NY, NY) * 2 + c, "expert": ex}

    def at_x(step):
        return {"dp": dp, "expert": lax.rem(x + step, NX) * NZ + z}

    def at_z(step):
        return {"dp": dp, "expert": x * NZ + lax.rem(z + step + NZ, NZ)}

    other = {"dp": y * 2 + 1 - c, "expert": ex}
    y_up, y_down = at_y(1), at_y(-1)
    z_up, z_down = at_z(1), at_z(-1)
    x_peers = [None] + [at_x(d) for d in range(1, NX)]

    barrier = pltpu.get_barrier_semaphore()
    greeted = [other, y_up, y_down, z_up, z_down] + x_peers[1:]
    for dev in greeted:
        pl.semaphore_signal(barrier, inc=1, device_id=dev, device_id_type=MESH)
    pl.semaphore_wait(barrier, len(greeted))

    copies = []

    def send(src, dst, dev):
        i = len(copies)
        copy = pltpu.make_async_remote_copy(
            src_ref=src, dst_ref=dst, send_sem=ssem.at[i], recv_sem=rsem.at[i],
            device_id=dev, device_id_type=MESH,
        )
        copies.append(copy)
        copy.start()
        return copy

    def zrows(step):
        return pl.ds(pl.multiple_of(lax.rem(z + step + NZ, NZ) * tok_rows, tok_rows), tok_rows)

    own = [tok_ref, cot_ref]
    ring = {}
    for a in (0, 1):
        ring[a, 1] = send(own[a], t.at[a, zrows(0)], z_up)
        ring[a, -1] = send(own[a], t.at[a, zrows(0)], z_down)
        if a == 0:
            ring[2, 1] = send(meta_ref, meta.at[z], z_up)
            ring[2, -1] = send(meta_ref, meta.at[z], z_down)

    mats = [wg_ref, wu_ref, wd_ref]

    def wrows(place, side, h):
        return pl.ds((place * 2 + side) * unit + h * half, half)

    wcopy = {}
    for m in range(3):
        for h in (0, 1):
            src = mats[m].at[pl.ds(h * half, half)]
            wcopy[m, 0, h] = send(src, w.at[m, wrows(0, 1, h)], other)
            g = 1 - h
            src_g = mats[m].at[pl.ds(g * half, half)]
            wcopy[m, 2, h] = send(src, w.at[m, wrows(2, 0, h)], y_up)
            wcopy[m, 1, g] = send(src_g, w.at[m, wrows(1, 0, g)], y_down)
    local = []
    for i, (src, dst) in enumerate(
        [(tok_ref, t.at[0, zrows(0)]), (cot_ref, t.at[1, zrows(0)]), (meta_ref, meta.at[z])]
        + [(mats[m], w.at[m, pl.ds(0, unit)]) for m in range(3)]
    ):
        copy = pltpu.make_async_copy(src, dst, lsem.at[i])
        copy.start()
        local.append(copy)

    wfwd = {}

    def forward_weights(m):
        for h in (0, 1):
            g = 1 - h
            wcopy[m, 2, h].wait_recv()
            if h == 0:
                wcopy[m, 3, 0] = send(w.at[m, wrows(2, 0, 0)], w.at[m, wrows(3, 0, 0)], y_up)
            wfwd[m, 2, h] = send(w.at[m, wrows(2, 0, h)], w.at[m, wrows(2, 1, h)], other)
            wcopy[m, 1, g].wait_recv()
            if g == 1:
                wcopy[m, 3, 1] = send(w.at[m, wrows(1, 0, 1)], w.at[m, wrows(3, 0, 1)], y_down)
            wfwd[m, 1, g] = send(w.at[m, wrows(1, 0, g)], w.at[m, wrows(1, 1, g)], other)

    def forward_last(m):
        for h in (0, 1):
            wcopy[m, 3, h].wait_recv()
            wfwd[m, 3, h] = send(w.at[m, wrows(3, 0, h)], w.at[m, wrows(3, 1, h)], other)

    hops = {(0, 1): 4, (0, -1): 3, (1, 1): 3, (1, -1): 4, (2, 1): 4, (2, -1): 3}

    def ring_step(a, step):
        for sign in (1, -1):
            if step <= hops[a, sign]:
                ring[a, sign].wait_recv()
                if step < hops[a, sign]:
                    dev = z_up if sign == 1 else z_down
                    if a == 2:
                        place = meta.at[lax.rem(z - sign * step + NZ, NZ)]
                    else:
                        place = t.at[a, zrows(-sign * step)]
                    ring[a, sign] = send(place, place, dev)

    for step in (1, 2, 3, 4):
        for a in (2, 0, 1):
            if (a, step) != (1, 4):
                ring_step(a, step)
        if step == 2:
            forward_weights(0)
    for copy in local[:3]:
        copy.wait()

    table = meta[0]
    for i in range(1, NZ):
        table = table + meta[i]
    count = NZ * tok_rows
    lane_of = lax.broadcasted_iota(jnp.int32, (count, count), 1)
    line_of = lax.broadcasted_iota(jnp.int32, (count, count), 0)
    before = ((lane_of >> 5) == (line_of >> 5)) & (line_of < lane_of)
    before = jnp.where(before, 1.0, 0.0).astype(BF)
    line8 = lax.broadcasted_iota(jnp.int32, (8, count), 0)
    base8 = ((lax.broadcasted_iota(jnp.int32, (8, count), 1) >> 5) * CAP).astype(F32)
    taken = jnp.zeros((8, count), F32)
    gates = []
    for d in range(NX):
        number = (lax.rem(x + d, NX) * NZ + z + 1).astype(F32)
        hit = jnp.where(table[0:8] == number, 1.0, 0.0)
        taken = jnp.where(line8 == d, jnp.sum(hit, axis=0, keepdims=True), taken)
        gates.append(jnp.sum(hit * table[8:16], axis=0, keepdims=True))
    place = base8 + mm(taken.astype(BF), before)
    place = jnp.where(taken > 0.5, place, -1.0)
    line_seg = lax.broadcasted_iota(jnp.int32, (seg, count), 0).astype(F32)
    weighted = []
    for d in range(NX):
        one = jnp.where(line_seg == place[d : d + 1], 1.0, 0.0)
        sel[pl.ds(d * seg, seg), :] = one.astype(BF)
        weighted.append(one * gates[d])
    weighted = jnp.concatenate(weighted, axis=0).T
    high = weighted.astype(BF)
    comb[0] = high
    comb[1] = (weighted - high.astype(F32)).astype(BF)

    xcopy = {}

    def pick(a):
        @pl.loop(0, 4)
        def _(i):
            cols = pl.ds(pl.multiple_of(i * (width // 4), width // 4), width // 4)
            got = mm(sel[...], t[a, :, cols]).astype(BF)
            rows[a, pl.ds(0, seg), cols] = got[0:seg]
            for d in range(1, NX):
                xs[a, d - 1, :, cols] = got[d * seg : (d + 1) * seg]

        for d in (2, 1, 3):
            xcopy[a, d] = send(xs.at[a, d - 1], rows.at[a, pl.ds((NX - d) * seg, seg)], x_peers[d])

    pick(0)
    ring_step(1, 4)
    pick(1)
    forward_weights(1)

    def first(row0, tiles, tile):
        @pl.loop(0, tiles)
        def _(i):
            span = pl.ds(pl.multiple_of(row0 + i * tile, 128), tile)
            into = pl.ds(pl.multiple_of(i * tile, 128), tile)
            gate = mm_nt(rows[0], w[0, span, :])
            up = mm_nt(rows[0], w[1, span, :])
            back = mm_nt(rows[1], w[2, span, :])
            sig = jax.nn.sigmoid(gate)
            silu = gate * sig
            hid[0, :, into] = (silu * up).astype(BF)
            hid[1, :, into] = (back * up * sig * (1.0 + gate * (1.0 - sig))).astype(BF)
            hid[2, :, into] = (back * silu).astype(BF)

    def second(row0, span, cols):
        both = pl.ds(row0, span)
        some = pl.ds(0, span)
        out = mm(hid[0, :, some], w[2, both, cols])
        grad = mm(hid[1, :, some], w[0, both, cols]) + mm(hid[2, :, some], w[1, both, cols])
        return out, grad

    pair = 2 * unit
    for d in range(1, NX):
        xcopy[0, d].wait_recv()
    forward_weights(2)
    for d in range(1, NX):
        xcopy[1, d].wait_recv()
    for m in range(3):
        local[3 + m].wait()
        for h in (0, 1):
            wcopy[m, 0, h].wait_recv()
    first(0, 1, pair)

    @pl.loop(0, 4)
    def _(i):
        cols = pl.ds(pl.multiple_of(i * (width // 4), width // 4), width // 4)
        out, grad = second(0, pair, cols)
        acc[0, :, cols] = out
        acc[1, :, cols] = grad

    forward_last(0)
    for m in range(3):
        for p in (1, 2):
            for h in (0, 1):
                wfwd[m, p, h].wait_recv()
    first(pair, 3, 256)
    forward_last(1)

    @pl.loop(0, 4)
    def _(i):
        cols = pl.ds(pl.multiple_of(i * (width // 4), width // 4), width // 4)
        out, grad = second(pair, 2 * pair, cols)
        acc[0, :, cols] += out
        acc[1, :, cols] += grad

    forward_last(2)
    for m in range(3):
        for h in (0, 1):
            wfwd[m, 3, h].wait_recv()
    first(3 * pair, 1, pair)

    ycopy = {}
    for j in range(CHUNKS):
        cols = pl.ds(j * cw, cw)
        for a, add in enumerate(second(3 * pair, pair, cols)):
            done = (acc[a, :, cols] + add).astype(BF)
            yr[j, a, pl.ds(0, seg), :] = done[0:seg]
            for d in (2, 1, 3):
                ys[j, a, d - 1] = done[d * seg : (d + 1) * seg]
                ycopy[j, a, d] = send(
                    ys.at[j, a, d - 1], yr.at[j, a, pl.ds((NX - d) * seg, seg)], x_peers[d]
                )

    outs = [out_a, out_b]
    for j in range(CHUNKS):
        for a in (0, 1):
            for d in range(1, NX):
                ycopy[j, a, d].wait_recv()
            part[a] = mm(comb[0], yr[j, a]) + mm(comb[1], yr[j, a])
        chain = {}
        for step in (1, 2, 3, 4):
            for a in (0, 1):
                for k, sign in enumerate((1, -1)):
                    far = hops[a, sign]
                    if step > far:
                        continue
                    term = part[a, zrows(sign * (far - step + 1)), :]
                    if step > 1:
                        chain[a, k].wait_recv()
                        term = term + rrecv[j, a, k, step - 2].astype(F32)
                    rsend[j, a, k, step - 1] = term.astype(BF)
                    chain[a, k] = send(
                        rsend.at[j, a, k, step - 1], rrecv.at[j, a, k, step - 1],
                        z_up if sign == 1 else z_down,
                    )
        for a in (0, 1):
            total = part[a, zrows(0), :]
            for k, sign in enumerate((1, -1)):
                chain[a, k].wait_recv()
                total = total + rrecv[j, a, k, hops[a, sign] - 1].astype(F32)
            outs[a][:, pl.ds(j * cw, cw)] = total.astype(BF)

    for copy in copies:
        copy.wait_send()


def shards(tokens, expert_ids, gate_weights, cotangent, w_gate, w_up, w_down):
    tok_rows, width = tokens.shape
    unit = w_gate.shape[1]
    z = lax.rem(lax.axis_index("expert"), NZ)
    meta = jnp.concatenate([expert_ids.T.astype(F32) + 1.0, gate_weights.T], axis=0)
    lane = lax.broadcasted_iota(jnp.int32, (16, NZ * tok_rows), 1)
    meta = jnp.where(lane // tok_rows == z, jnp.tile(meta, (1, NZ)), 0.0)
    seg = NZ * CAP
    slots = NX * seg
    hidden = NY * 2 * unit
    cw = width // CHUNKS
    n_copies = 42 + 21 + 6 + CHUNKS * (6 + 14)
    hbm = pl.BlockSpec(memory_space=pl.ANY)
    vmem = pl.BlockSpec(memory_space=pltpu.VMEM)
    result = jax.ShapeDtypeStruct((tok_rows, width), BF)
    return pl.pallas_call(
        kernel,
        out_shape=(result, result),
        in_specs=[hbm] * 6,
        out_specs=(vmem, vmem),
        scratch_shapes=[
            pltpu.VMEM((3, hidden, width), BF),
            pltpu.VMEM((2, NZ * tok_rows, width), BF),
            pltpu.VMEM((NZ, 16, NZ * tok_rows), F32),
            pltpu.VMEM((slots, NZ * tok_rows), BF),
            pltpu.VMEM((2, NZ * tok_rows, slots), BF),
            pltpu.VMEM((2, NX - 1, seg, width), BF),
            pltpu.VMEM((2, slots, width), BF),
            pltpu.VMEM((3, slots, 4 * unit), BF),
            pltpu.VMEM((2, slots, width), F32),
            pltpu.VMEM((CHUNKS, 2, NX - 1, seg, cw), BF),
            pltpu.VMEM((CHUNKS, 2, slots, cw), BF),
            pltpu.VMEM((2, NZ * tok_rows, cw), F32),
            pltpu.VMEM((CHUNKS, 2, 2, 4, tok_rows, cw), BF),
            pltpu.VMEM((CHUNKS, 2, 2, 4, tok_rows, cw), BF),
            pltpu.SemaphoreType.DMA((n_copies,)),
            pltpu.SemaphoreType.DMA((n_copies,)),
            pltpu.SemaphoreType.DMA((6,)),
        ],
        compiler_params=pltpu.CompilerParams(
            collective_id=0, has_side_effects=True, vmem_limit_bytes=60 * 1024 * 1024
        ),
    )(tokens, cotangent, meta, w_gate[0], w_up[0], w_down[0])


def solution(mesh):
    both = P(("dp", "expert"), None)
    weights = P("expert", "dp", None)
    return jax.shard_map(
        shards,
        mesh=mesh,
        in_specs=(both, both, both, both, weights, weights, weights),
        out_specs=(both, both),
        check_vma=False,
    )
```

```python
import functools

import jax
import jax.numpy as jnp
from jax import lax
from jax.experimental import pallas as pl
from jax.experimental.pallas import tpu as pltpu
from jax.sharding import PartitionSpec as P

MESH = pl.DeviceIdType.MESH
NX, NY, NZ = 4, 4, 8
CAP = 12
CHUNKS = 4
NT = (((1,), (1,)), ((), ()))
BF = jnp.bfloat16
F32 = jnp.float32


def mm(a, b):
    return jnp.dot(a, b, preferred_element_type=F32)


def mm_nt(a, b):
    return lax.dot_general(a, b, NT, preferred_element_type=F32)


def kernel(
    tok_ref, cot_ref, meta_ref, wg_ref, wu_ref, wd_ref, out_a, out_b,
    w, wd, t, meta, sel, comb, xs, rows, hid, fac, back, grads, ys, yr, part, rsend, rrecv,
    ssem, rsem, lsem,
):
    dp, ex = lax.axis_index("dp"), lax.axis_index("expert")
    y, c = dp // 2, lax.rem(dp, 2)
    x, z = ex // NZ, lax.rem(ex, NZ)
    tok_rows, width = tok_ref.shape
    unit = wg_ref.shape[0]
    half = unit // 2
    seg = NZ * CAP
    cw = width // CHUNKS
    hidden = 2 * NY * unit

    def at_y(step):
        return {"dp": lax.rem(y + step + NY, NY) * 2 + c, "expert": ex}

    def at_x(step):
        return {"dp": dp, "expert": lax.rem(x + step, NX) * NZ + z}

    def at_z(step):
        return {"dp": dp, "expert": x * NZ + lax.rem(z + step + NZ, NZ)}

    other = {"dp": y * 2 + 1 - c, "expert": ex}
    y_up, y_down = at_y(1), at_y(-1)
    z_dev = {1: at_z(1), -1: at_z(-1)}
    x_peers = [None] + [at_x(d) for d in range(1, NX)]

    barrier = pltpu.get_barrier_semaphore()
    greeted = [other, y_up, y_down, z_dev[1], z_dev[-1]] + x_peers[1:]
    for dev in greeted:
        pl.semaphore_signal(barrier, inc=1, device_id=dev, device_id_type=MESH)
    pl.semaphore_wait(barrier, len(greeted))

    copies = []

    def send(src, dst, dev):
        i = len(copies)
        copy = pltpu.make_async_remote_copy(
            src_ref=src, dst_ref=dst, send_sem=ssem.at[i], recv_sem=rsem.at[i],
            device_id=dev, device_id_type=MESH,
        )
        copies.append(copy)
        copy.start()
        return copy

    def zrows(step):
        return pl.ds(pl.multiple_of(lax.rem(z + step + NZ, NZ) * tok_rows, tok_rows), tok_rows)

    own = [tok_ref, cot_ref, meta_ref]
    hops = {(0, 1): 4, (0, -1): 3, (1, 1): 3, (1, -1): 4, (2, 1): 4, (2, -1): 3}
    ring = {}

    def zplace(a, step):
        if a == 2:
            return meta.at[lax.rem(z + step + NZ, NZ)]
        return t.at[a, zrows(step)]

    def ring_start(a):
        for sign in (1, -1):
            ring[a, sign] = send(own[a], zplace(a, 0), z_dev[sign])

    def ring_step(a, step):
        for sign in (1, -1):
            if step <= hops[a, sign]:
                ring[a, sign].wait_recv()
                if step < hops[a, sign]:
                    place = zplace(a, -sign * step)
                    ring[a, sign] = send(place, place, z_dev[sign])

    mats = [wg_ref, wu_ref, wd_ref]

    def wrows(place, side, h=None):
        if h is None:
            return pl.ds((place * 2 + side) * unit, unit)
        return pl.ds((place * 2 + side) * unit + h * half, half)

    wcopy, wfwd = {}, {}

    def issue(k):
        if k < 4:
            m, h = k // 2, k % 2
            g = 1 - h
            wcopy[m, 2, h] = send(mats[m].at[pl.ds(h * half, half)], w.at[m, wrows(2, 0, h)], y_up)
            wcopy[m, 1, g] = send(mats[m].at[pl.ds(g * half, half)], w.at[m, wrows(1, 0, g)], y_down)
        elif k < 6:
            m = k - 4
            wcopy[m, 3, 0] = send(w.at[m, wrows(2, 0, 0)], w.at[m, wrows(3, 0, 0)], y_up)
            wcopy[m, 3, 1] = send(w.at[m, wrows(1, 0, 1)], w.at[m, wrows(3, 0, 1)], y_down)
        elif k < 6 + CHUNKS:
            j = k - 6
            src = wd_ref.at[:, pl.ds(j * cw, cw)]
            wcopy[2, 2, j] = send(src, wd.at[j, wrows(2, 0)], y_up)
            wcopy[2, 1, j] = send(src, wd.at[j, wrows(1, 0)], y_down)

    def hand_over(m, p, h):
        wcopy[m, p, h].wait_recv()
        ref = w.at[m, wrows(p, 0, h)]
        wfwd[m, p, h] = send(ref, w.at[m, wrows(p, 1, h)], other)

    def event(k):
        if k < 4:
            m, h = k // 2, k % 2
            hand_over(m, 2, h)
            hand_over(m, 1, 1 - h)
        else:
            for h in (0, 1):
                hand_over(k - 4, 3, h)
        issue(k + 3)

    def event_down(j):
        for p, to, h, dev in ((2, 3, 0, y_up), (1, 3, 1, y_down)):
            wcopy[2, p, j].wait_recv()
            wcopy[2, 3, j, h] = send(wd.at[j, wrows(p, 0, h)], wd.at[j, wrows(3, 0, h)], dev)
            wfwd[2, p, j] = send(wd.at[j, wrows(p, 0)], wd.at[j, wrows(p, 1)], other)
        issue(9 + j)

    def event_last(j):
        for h in (0, 1):
            wcopy[2, 3, j, h].wait_recv()
            wfwd[2, 3, j, h] = send(wd.at[j, wrows(3, 0, h)], wd.at[j, wrows(3, 1, h)], other)

    ring_start(2)
    ring_start(0)
    for k in range(3):
        issue(k)
    local = []

    def local_copy(src, dst):
        copy = pltpu.make_async_copy(src, dst, lsem.at[len(local)])
        copy.start()
        local.append(copy)

    for a in range(3):
        local_copy(own[a], zplace(a, 0))
    for m in (0, 1):
        local_copy(mats[m], w.at[m, wrows(0, 0)])
        wfwd[m, 0] = send(mats[m], w.at[m, wrows(0, 1)], other)
    for j in range(CHUNKS):
        src = wd_ref.at[:, pl.ds(j * cw, cw)]
        local_copy(src, wd.at[j, wrows(0, 0)])
        wfwd[2, 0, j] = send(src, wd.at[j, wrows(0, 1)], other)

    ring_step(2, 1)
    ring_step(0, 1)
    ring_start(1)
    ring_step(2, 2)
    ring_step(0, 2)
    ring_step(1, 1)
    event(0)
    ring_step(2, 3)
    ring_step(0, 3)
    ring_step(1, 2)
    ring_step(2, 4)
    ring_step(0, 4)
    for copy in local[:3]:
        copy.wait()

    table = meta[0]
    for i in range(1, NZ):
        table = table + meta[i]
    count = NZ * tok_rows
    lane_of = lax.broadcasted_iota(jnp.int32, (count, count), 1)
    line_of = lax.broadcasted_iota(jnp.int32, (count, count), 0)
    before = ((lane_of >> 5) == (line_of >> 5)) & (line_of < lane_of)
    before = jnp.where(before, 1.0, 0.0).astype(BF)
    line8 = lax.broadcasted_iota(jnp.int32, (8, count), 0)
    base8 = ((lax.broadcasted_iota(jnp.int32, (8, count), 1) >> 5) * CAP).astype(F32)
    taken = jnp.zeros((8, count), F32)
    gates = []
    for d in range(NX):
        number = (lax.rem(x + d, NX) * NZ + z + 1).astype(F32)
        hit = jnp.where(table[0:8] == number, 1.0, 0.0)
        taken = jnp.where(line8 == d, jnp.sum(hit, axis=0, keepdims=True), taken)
        gates.append(jnp.sum(hit * table[8:16], axis=0, keepdims=True))
    place = base8 + mm(taken.astype(BF), before)
    place = jnp.where(taken > 0.5, place, -1.0)
    line_seg = lax.broadcasted_iota(jnp.int32, (seg, count), 0).astype(F32)
    weighted = []
    for d in range(NX):
        one = jnp.where(line_seg == place[d : d + 1], 1.0, 0.0)
        sel[pl.ds(d * seg, seg), :] = one.astype(BF)
        weighted.append(one * gates[d])

    xcopy = {}

    def pick(a):
        @pl.loop(0, 4)
        def _(i):
            cols = pl.ds(pl.multiple_of(i * (width // 4), width // 4), width // 4)
            got = mm(sel[...], t[a, :, cols]).astype(BF)
            rows[a, pl.ds(0, seg), cols] = got[0:seg]
            for d in range(1, NX):
                xs[a, d - 1, :, cols] = got[d * seg : (d + 1) * seg]

    def send_rows(a):
        for d in (2, 1, 3):
            xcopy[a, d] = send(xs.at[a, d - 1], rows.at[a, pl.ds((NX - d) * seg, seg)], x_peers[d])

    pick(0)
    send_rows(0)
    event(1)
    ring_step(1, 3)
    weighted = jnp.concatenate(weighted, axis=0).T
    high = weighted.astype(BF)
    comb[0] = high
    comb[1] = (weighted - high.astype(F32)).astype(BF)
    ring_step(1, 4)
    event(2)
    pick(1)
    event(3)
    for d in range(1, NX):
        xcopy[0, d].wait_recv()
    send_rows(1)

    def first(row0, tiles, tile):
        @pl.loop(0, tiles)
        def _(i):
            span = pl.ds(pl.multiple_of(row0 + i * tile, 128), tile)
            gate = mm_nt(rows[0], w[0, span, :])
            up = mm_nt(rows[0], w[1, span, :])
            sig = jax.nn.sigmoid(gate)
            silu = gate * sig
            hid[:, span] = (silu * up).astype(BF)
            fac[0, :, span] = up * sig * (1.0 + gate * (1.0 - sig))
            fac[1, :, span] = silu

    pair = 2 * unit
    for m in (0, 1):
        local[3 + m].wait()
        wfwd[m, 0].wait_recv()
    first(0, 1, pair)
    event(4)
    for m in (0, 1):
        for p in (1, 2):
            for h in (0, 1):
                wfwd[m, p, h].wait_recv()
    first(pair, 3, 256)
    event(5)
    for m in (0, 1):
        for h in (0, 1):
            wfwd[m, 3, h].wait_recv()
    first(3 * pair, 1, pair)

    ycopy, chain = {}, {}
    outs = [out_a, out_b]

    def send_back(a, j, done):
        yr[a, j, pl.ds(0, seg), :] = done[0:seg]
        for d in (2, 1, 3):
            ys[a, j, d - 1] = done[d * seg : (d + 1) * seg]
            ycopy[a, j, d] = send(
                ys.at[a, j, d - 1], yr.at[a, j, pl.ds((NX - d) * seg, seg)], x_peers[d]
            )

    def gather_back(a, j):
        for d in range(1, NX):
            ycopy[a, j, d].wait_recv()
        part[a, j] = mm(comb[0], yr[a, j]) + mm(comb[1], yr[a, j])

    def sum_step(a, j, step):
        if step == 5:
            total = part[a, j, zrows(0), :]
            for k, sign in enumerate((1, -1)):
                chain[a, j, k].wait_recv()
                total = total + rrecv[a, j, k, hops[a, sign] - 1].astype(F32)
            outs[a][:, pl.ds(j * cw, cw)] = total.astype(BF)
            return
        for k, sign in enumerate((1, -1)):
            far = hops[a, sign]
            if step > far:
                continue
            term = part[a, j, zrows(sign * (far - step + 1)), :]
            if step > 1:
                chain[a, j, k].wait_recv()
                term = term + rrecv[a, j, k, step - 2].astype(F32)
            rsend[a, j, k, step - 1] = term.astype(BF)
            chain[a, j, k] = send(
                rsend.at[a, j, k, step - 1], rrecv.at[a, j, k, step - 1], z_dev[sign]
            )

    def tick(q):
        if q < 2 * CHUNKS:
            gather_back(q // CHUNKS, q % CHUNKS)
            sum_step(q // CHUNKS, q % CHUNKS, 1)
        for i in range(1, 5):
            if 0 <= q - i < 2 * CHUNKS:
                sum_step((q - i) // CHUNKS, (q - i) % CHUNKS, 1 + i)

    def down_ready(j):
        local[5 + j].wait()
        wfwd[2, 0, j].wait_recv()
        for p in (1, 2):
            wfwd[2, p, j].wait_recv()
        for h in (0, 1):
            wfwd[2, 3, j, h].wait_recv()

    for d in range(1, NX):
        xcopy[1, d].wait_recv()
    event_down(0)
    for j in range(CHUNKS):
        if j + 1 < CHUNKS:
            event_down(j + 1)
        event_last(j)
        down_ready(j)
        send_back(0, j, mm(hid[...], wd[j]).astype(BF))

        @pl.loop(0, hidden // 256)
        def _(i):
            span = pl.ds(pl.multiple_of(i * 256, 256), 256)
            term = mm_nt(rows[1, :, pl.ds(j * cw, cw)], wd[j, span, :])
            if j > 0:
                term = term + back[:, span]
            if j + 1 < CHUNKS:
                back[:, span] = term
            else:
                grads[0, :, span] = (term * fac[0, :, span]).astype(BF)
                grads[1, :, span] = (term * fac[1, :, span]).astype(BF)

        if j > 0:
            tick(j - 1)
    for j in range(CHUNKS):
        cols = pl.ds(j * cw, cw)
        done = mm(grads[0], w[0, :, cols]) + mm(grads[1], w[1, :, cols])
        send_back(1, j, done.astype(BF))
        if j > 0:
            tick(CHUNKS + j - 2)
    for q in range(2 * CHUNKS - 2, 2 * CHUNKS + 4):
        tick(q)

    for copy in copies:
        copy.wait_send()


def shards(tokens, expert_ids, gate_weights, cotangent, w_gate, w_up, w_down):
    tok_rows, width = tokens.shape
    unit = w_gate.shape[1]
    z = lax.rem(lax.axis_index("expert"), NZ)
    meta = jnp.concatenate([expert_ids.T.astype(F32) + 1.0, gate_weights.T], axis=0)
    lane = lax.broadcasted_iota(jnp.int32, (16, NZ * tok_rows), 1)
    meta = jnp.where(lane // tok_rows == z, jnp.tile(meta, (1, NZ)), 0.0)
    seg = NZ * CAP
    slots = NX * seg
    hidden = NY * 2 * unit
    cw = width // CHUNKS
    n_copies = 26 + 9 * CHUNKS + 21 + 6 + 2 * CHUNKS * (3 + 7)
    hbm = pl.BlockSpec(memory_space=pl.ANY)
    vmem = pl.BlockSpec(memory_space=pltpu.VMEM)
    result = jax.ShapeDtypeStruct((tok_rows, width), BF)
    return pl.pallas_call(
        kernel,
        out_shape=(result, result),
        in_specs=[hbm] * 6,
        out_specs=(vmem, vmem),
        scratch_shapes=[
            pltpu.VMEM((2, hidden, width), BF),
            pltpu.VMEM((CHUNKS, hidden, cw), BF),
            pltpu.VMEM((2, NZ * tok_rows, width), BF),
            pltpu.VMEM((NZ, 16, NZ * tok_rows), F32),
            pltpu.VMEM((slots, NZ * tok_rows), BF),
            pltpu.VMEM((2, NZ * tok_rows, slots), BF),
            pltpu.VMEM((2, NX - 1, seg, width), BF),
            pltpu.VMEM((2, slots, width), BF),
            pltpu.VMEM((slots, hidden), BF),
            pltpu.VMEM((2, slots, hidden), F32),
            pltpu.VMEM((slots, hidden), F32),
            pltpu.VMEM((2, slots, hidden), BF),
            pltpu.VMEM((2, CHUNKS, NX - 1, seg, cw), BF),
            pltpu.VMEM((2, CHUNKS, slots, cw), BF),
            pltpu.VMEM((2, CHUNKS, NZ * tok_rows, cw), F32),
            pltpu.VMEM((2, CHUNKS, 2, 4, tok_rows, cw), BF),
            pltpu.VMEM((2, CHUNKS, 2, 4, tok_rows, cw), BF),
            pltpu.SemaphoreType.DMA((n_copies,)),
            pltpu.SemaphoreType.DMA((n_copies,)),
            pltpu.SemaphoreType.DMA((5 + CHUNKS,)),
        ],
        compiler_params=pltpu.CompilerParams(
            collective_id=0, has_side_effects=True, vmem_limit_bytes=60 * 1024 * 1024
        ),
    )(tokens, cotangent, meta, w_gate[0], w_up[0], w_down[0])


def solution(mesh):
    both = P(("dp", "expert"), None)
    weights = P("expert", "dp", None)
    return jax.shard_map(
        shards,
        mesh=mesh,
        in_specs=(both, both, both, both, weights, weights, weights),
        out_specs=(both, both),
        check_vma=False,
    )
```

```python
import functools

import jax
import jax.numpy as jnp
from jax import lax
from jax.experimental import pallas as pl
from jax.experimental.pallas import tpu as pltpu
from jax.sharding import PartitionSpec as P

MESH = pl.DeviceIdType.MESH
NX, NY, NZ = 4, 4, 8
CAP = 12
COLS = 256
PARTS_A = (1, 2, 2, 2, 1)
PARTS_B = (2, 2, 2, 1, 1)
RINGED = 3
NT = (((1,), (1,)), ((), ()))
BF = jnp.bfloat16
F32 = jnp.float32


def mm(a, b):
    return jnp.dot(a, b, preferred_element_type=F32)


def mm_nt(a, b):
    return lax.dot_general(a, b, NT, preferred_element_type=F32)


def kernel(
    tok_ref, cot_ref, ids_ref, gate_ref, wg_ref, wu_ref, wd_ref, out_a, out_b,
    w, t, meta, ids_in, gates_in, sel, comb, xs, rows, hid, fac, back, grads, ys, yr, part, rsend, rrecv, dsend, drecv,
    ssem, rsem, lsem,
):
    dp, ex = lax.axis_index("dp"), lax.axis_index("expert")
    y, c = dp // 2, lax.rem(dp, 2)
    x, z = ex // NZ, lax.rem(ex, NZ)
    tok_rows, width = tok_ref.shape
    unit = wg_ref.shape[0]
    half = unit // 2
    seg = NZ * CAP
    hidden = 2 * NY * unit

    def at_y(step):
        return {"dp": lax.rem(y + step + NY, NY) * 2 + c, "expert": ex}

    def at_x(step):
        return {"dp": dp, "expert": lax.rem(x + step, NX) * NZ + z}

    def at_z(step):
        return {"dp": dp, "expert": x * NZ + lax.rem(z + step + NZ, NZ)}

    other = {"dp": y * 2 + 1 - c, "expert": ex}
    y_up, y_down = at_y(1), at_y(-1)
    z_dev = {1: at_z(1), -1: at_z(-1)}
    z_peers = [None] + [at_z(s) for s in range(1, NZ)]
    x_peers = [None] + [at_x(d) for d in range(1, NX)]

    barrier = pltpu.get_barrier_semaphore()
    greeted = [other, y_up, y_down] + z_peers[1:] + x_peers[1:]
    for dev in greeted:
        pl.semaphore_signal(barrier, inc=1, device_id=dev, device_id_type=MESH)

    local = []

    def local_copy(src, dst):
        copy = pltpu.make_async_copy(src, dst, lsem.at[len(local)])
        copy.start()
        local.append(copy)

    local_copy(ids_ref, ids_in)
    local_copy(gate_ref, gates_in)
    lanes = NZ * tok_rows
    token_lane = lax.broadcasted_iota(jnp.int32, (tok_rows, lanes), 0) + z * tok_rows
    spread = token_lane == lax.broadcasted_iota(jnp.int32, (tok_rows, lanes), 1)
    spread = jnp.where(spread, 1.0, 0.0).astype(BF)
    local[0].wait()
    local[1].wait()
    meta[z, 0:8] = mm((ids_in[...].astype(F32) + 1.0).astype(BF), spread)
    rest = gates_in[...]
    spread_gates = jnp.zeros((8, lanes), F32)
    for _ in range(3):
        piece = rest.astype(BF)
        spread_gates = spread_gates + mm(piece, spread)
        rest = rest - piece.astype(F32)
    meta[z, 8:16] = spread_gates
    pl.semaphore_wait(barrier, len(greeted))

    copies = []

    def send(src, dst, dev):
        i = len(copies)
        copy = pltpu.make_async_remote_copy(
            src_ref=src, dst_ref=dst, send_sem=ssem.at[i], recv_sem=rsem.at[i],
            device_id=dev, device_id_type=MESH,
        )
        copies.append(copy)
        copy.start()
        return copy

    def zrows(step):
        return pl.ds(pl.multiple_of(lax.rem(z + step + NZ, NZ) * tok_rows, tok_rows), tok_rows)

    own = [tok_ref, cot_ref, meta.at[z]]
    hops = {(0, 1): 4, (0, -1): 3, (1, 1): 3, (1, -1): 4, (2, 1): 4, (2, -1): 3}
    ring = {}

    def zplace(a, step):
        if a == 2:
            return meta.at[lax.rem(z + step + NZ, NZ)]
        return t.at[a, zrows(step)]

    def ring_start(a):
        for sign in (1, -1):
            ring[a, sign] = send(own[a], zplace(a, 0), z_dev[sign])

    def ring_step(a, step):
        for sign in (1, -1):
            if step <= hops[a, sign]:
                ring[a, sign].wait_recv()
                if step < hops[a, sign]:
                    place = zplace(a, -sign * step)
                    ring[a, sign] = send(place, place, z_dev[sign])

    mats = [wg_ref, wu_ref, wd_ref]

    def wrows(place, side, h=None):
        if h is None:
            return pl.ds((place * 2 + side) * unit, unit)
        return pl.ds((place * 2 + side) * unit + h * half, half)

    wcopy, wfwd = {}, {}
    dcols = [pl.ds(sum(PARTS_A[:j]) * COLS, PARTS_A[j] * COLS) for j in range(len(PARTS_A))]

    def issue(k):
        if k < 4:
            m, h = k // 2, k % 2
            g = 1 - h
            wcopy[m, 2, h] = send(mats[m].at[pl.ds(h * half, half)], w.at[m, wrows(2, 0, h)], y_up)
            wcopy[m, 1, g] = send(mats[m].at[pl.ds(g * half, half)], w.at[m, wrows(1, 0, g)], y_down)
        elif k < 6:
            m = k - 4
            wcopy[m, 3, 0] = send(w.at[m, wrows(2, 0, 0)], w.at[m, wrows(3, 0, 0)], y_up)
            wcopy[m, 3, 1] = send(w.at[m, wrows(1, 0, 1)], w.at[m, wrows(3, 0, 1)], y_down)
        elif k < 6 + len(PARTS_A):
            j = k - 6
            src = wd_ref.at[:, dcols[j]]
            wcopy[2, 2, j] = send(src, w.at[2, wrows(2, 0), dcols[j]], y_up)
            wcopy[2, 1, j] = send(src, w.at[2, wrows(1, 0), dcols[j]], y_down)

    def hand_over(m, p, h):
        wcopy[m, p, h].wait_recv()
        ref = w.at[m, wrows(p, 0, h)]
        wfwd[m, p, h] = send(ref, w.at[m, wrows(p, 1, h)], other)

    def event(k):
        if k < 4:
            m, h = k // 2, k % 2
            hand_over(m, 2, h)
            hand_over(m, 1, 1 - h)
        else:
            for h in (0, 1):
                hand_over(k - 4, 3, h)

    def event_down(j):
        for p, h, dev in ((2, 0, y_up), (1, 1, y_down)):
            wcopy[2, p, j].wait_recv()
            wcopy[2, 3, j, h] = send(
                w.at[2, wrows(p, 0, h), dcols[j]], w.at[2, wrows(3, 0, h), dcols[j]], dev
            )
        issue(8 + j)
        for p in (2, 1):
            wfwd[2, p, j] = send(w.at[2, wrows(p, 0), dcols[j]], w.at[2, wrows(p, 1), dcols[j]], other)

    def event_last(j):
        for h in (0, 1):
            wcopy[2, 3, j, h].wait_recv()
            wfwd[2, 3, j, h] = send(
                w.at[2, wrows(3, 0, h), dcols[j]], w.at[2, wrows(3, 1, h), dcols[j]], other
            )

    ring_start(2)
    ring_start(0)
    for k in range(4):
        issue(k)
    for a in (0, 1):
        local_copy(own[a], zplace(a, 0))
    for m in range(3):
        local_copy(mats[m], w.at[m, wrows(0, 0)])
        wfwd[m, 0] = send(mats[m], w.at[m, wrows(0, 1)], other)

    ring_step(2, 1)
    ring_step(0, 1)
    ring_start(1)
    ring_step(2, 2)
    ring_step(0, 2)
    ring_step(1, 1)
    ring_step(2, 3)
    ring_step(0, 3)
    ring_step(1, 2)
    ring_step(2, 4)
    ring_step(0, 4)
    for copy in local[2:4]:
        copy.wait()

    table = meta[0]
    for i in range(1, NZ):
        table = table + meta[i]
    count = NZ * tok_rows
    lane_of = lax.broadcasted_iota(jnp.int32, (count, count), 1)
    line_of = lax.broadcasted_iota(jnp.int32, (count, count), 0)
    before = ((lane_of >> 5) == (line_of >> 5)) & (line_of < lane_of)
    before = jnp.where(before, 1.0, 0.0).astype(BF)
    line8 = lax.broadcasted_iota(jnp.int32, (8, count), 0)
    base8 = ((lax.broadcasted_iota(jnp.int32, (8, count), 1) >> 5) * CAP).astype(F32)
    taken = jnp.zeros((8, count), F32)
    gates = []
    for d in range(NX):
        number = (lax.rem(x + d, NX) * NZ + z + 1).astype(F32)
        hit = jnp.where(table[0:8] == number, 1.0, 0.0)
        taken = jnp.where(line8 == d, jnp.sum(hit, axis=0, keepdims=True), taken)
        gates.append(jnp.sum(hit * table[8:16], axis=0, keepdims=True))
    place = base8 + mm(taken.astype(BF), before)
    place = jnp.where(taken > 0.5, place, -1.0)
    line_seg = lax.broadcasted_iota(jnp.int32, (seg, count), 0).astype(F32)
    weighted = []
    for d in range(NX):
        one = jnp.where(line_seg == place[d : d + 1], 1.0, 0.0)
        sel[pl.ds(d * seg, seg), :] = one.astype(BF)
        weighted.append(one * gates[d])

    xcopy = {}

    def pick(a):
        @pl.loop(0, 4)
        def _(i):
            cols = pl.ds(pl.multiple_of(i * (width // 4), width // 4), width // 4)
            got = mm(sel[...], t[a, :, cols]).astype(BF)
            rows[a, pl.ds(0, seg), cols] = got[0:seg]
            for d in range(1, NX):
                xs[a, d - 1, :, cols] = got[d * seg : (d + 1) * seg]

    def send_rows(a):
        for d in (2, 1, 3):
            xcopy[a, d] = send(xs.at[a, d - 1], rows.at[a, pl.ds((NX - d) * seg, seg)], x_peers[d])

    pick(0)
    send_rows(0)
    event(0)
    issue(4)
    event(1)
    ring_step(1, 3)
    event(2)
    for k in range(5, 8):
        issue(k)
    weighted = jnp.concatenate(weighted, axis=0).T
    high = weighted.astype(BF)
    comb[0] = high
    comb[1] = (weighted - high.astype(F32)).astype(BF)
    ring_step(1, 4)
    pick(1)
    send_rows(1)
    event(3)
    event(4)
    for d in range(1, NX):
        xcopy[0, d].wait_recv()

    def first(row0, tiles, tile):
        @pl.loop(0, tiles)
        def _(i):
            span = pl.ds(pl.multiple_of(row0 + i * tile, 128), tile)
            gate = mm_nt(rows[0], w[0, span, :])
            up = mm_nt(rows[0], w[1, span, :])
            sig = jax.nn.sigmoid(gate)
            silu = gate * sig
            hid[:, span] = (silu * up).astype(BF)
            fac[0, :, span] = up * sig * (1.0 + gate * (1.0 - sig))
            fac[1, :, span] = silu

    pair = 2 * unit
    for m in (0, 1):
        local[4 + m].wait()
        wfwd[m, 0].wait_recv()
    first(0, 1, pair)
    for m in (0, 1):
        for p in (1, 2):
            for h in (0, 1):
                wfwd[m, p, h].wait_recv()
    first(pair, 3, 256)
    event(5)
    for m in (0, 1):
        for h in (0, 1):
            wfwd[m, 3, h].wait_recv()
    first(3 * pair, 1, pair)

    chunks = []
    for a, parts in enumerate((PARTS_A, PARTS_B)):
        for i, n in enumerate(parts):
            chunks.append((a, sum(parts[:i]), n, a == 0 or i < RINGED))
    ycopy, chain = {}, {}
    outs = [out_a, out_b]

    def send_back(q, done):
        a, u, n, _ = chunks[q]
        for d in (2, 1, 3):
            for i in range(n):
                ys[a, d - 1, u + i] = done[d * seg : (d + 1) * seg, i * COLS : (i + 1) * COLS]
            ycopy[q, d] = send(
                ys.at[a, d - 1, pl.ds(u, n)],
                yr.at[a, pl.ds(u, n), pl.ds((NX - d) * seg, seg)],
                x_peers[d],
            )
        for i in range(n):
            yr[a, u + i, pl.ds(0, seg), :] = done[0:seg, i * COLS : (i + 1) * COLS]

    def gather_back(q):
        a, u, n, _ = chunks[q]
        for d in range(1, NX):
            ycopy[q, d].wait_recv()
        for i in range(u, u + n):
            part[a, i] = mm(comb[0], yr[a, i]) + mm(comb[1], yr[a, i])

    def direct_sum(q, step):
        a, u, n, _ = chunks[q]
        if step == 1:
            for s in (4, 3, 5, 2, 6, 1, 7):
                dsend[s - 1, pl.ds(u, n)] = part[a, pl.ds(u, n), zrows(s), :].astype(BF)
                chain[q, s] = send(
                    dsend.at[s - 1, pl.ds(u, n)], drecv.at[s - 1, pl.ds(u, n)], z_peers[s]
                )
            return
        for s in range(1, NZ):
            chain[q, s].wait_recv()
        for i in range(u, u + n):
            total = part[a, i, zrows(0), :]
            for s in range(1, NZ):
                total = total + drecv[s - 1, i].astype(F32)
            outs[a][:, pl.ds(i * COLS, COLS)] = total.astype(BF)

    def ring_sum(q, step):
        a, u, n, _ = chunks[q]
        if step == 5:
            for k in (0, 1):
                chain[q, k].wait_recv()
            for i in range(u, u + n):
                total = part[a, i, zrows(0), :]
                for k, sign in enumerate((1, -1)):
                    total = total + rrecv[a, k, hops[a, sign] - 1, i].astype(F32)
                outs[a][:, pl.ds(i * COLS, COLS)] = total.astype(BF)
            return
        for k, sign in enumerate((1, -1)):
            far = hops[a, sign]
            if step > far:
                continue
            some = pl.ds(u, n)
            term = part[a, some, zrows(sign * (far - step + 1)), :]
            if step > 1:
                chain[q, k].wait_recv()
                term = term + rrecv[a, k, step - 2, some].astype(F32)
            rsend[a, k, step - 1, some] = term.astype(BF)
            chain[q, k] = send(
                rsend.at[a, k, step - 1, some], rrecv.at[a, k, step - 1, some], z_dev[sign]
            )

    begun = []

    def tick(*starting):
        for q, age in begun:
            if chunks[q][3] and age <= 5:
                ring_sum(q, age)
        for q, age in begun:
            if not chunks[q][3] and age == 3:
                direct_sum(q, 2)
        begun[:] = [(q, age + 1) for q, age in begun]
        for q in starting:
            gather_back(q)
            (ring_sum if chunks[q][3] else direct_sum)(q, 1)
            begun.append((q, 2))

    def layer_chunk(j):
        if j == 0:
            local[6].wait()
            wfwd[2, 0].wait_recv()
        for p in (1, 2):
            wfwd[2, p, j].wait_recv()
        for h in (0, 1):
            wfwd[2, 3, j, h].wait_recv()
        send_back(j, mm(hid[...], w[2, :, dcols[j]]).astype(BF))

    def back_chunk(j):
        @pl.loop(0, hidden // 256)
        def _(i):
            span = pl.ds(pl.multiple_of(i * 256, 256), 256)
            term = mm_nt(rows[1, :, dcols[j]], w[2, span, dcols[j]])
            if j > 0:
                term = term + back[:, span]
            if j + 1 < len(PARTS_A):
                back[:, span] = term
            else:
                grads[0, :, span] = (term * fac[0, :, span]).astype(BF)
                grads[1, :, span] = (term * fac[1, :, span]).astype(BF)

    def grad_chunk(q):
        _, u, n, _ = chunks[q]
        cols = pl.ds(u * COLS, n * COLS)
        done = mm(grads[0], w[0, :, cols]) + mm(grads[1], w[1, :, cols])
        send_back(q, done.astype(BF))

    event_down(0)
    event_down(1)
    event_last(0)
    layer_chunk(0)
    for d in range(1, NX):
        xcopy[1, d].wait_recv()
    back_chunk(0)
    event_down(2)
    event_last(1)
    layer_chunk(1)
    back_chunk(1)
    tick(0)
    event_down(3)
    event_last(2)
    layer_chunk(2)
    event_down(4)
    back_chunk(2)
    tick(1)
    event_last(3)
    layer_chunk(3)
    event_last(4)
    back_chunk(3)
    layer_chunk(4)
    settled = len(copies)
    back_chunk(4)
    grad_chunk(5)
    grad_chunk(6)
    grad_chunk(7)
    tick(2, 3, 4)
    grad_chunk(8)
    grad_chunk(9)
    tick(5)
    for copy in copies[:settled]:
        copy.wait_send()
    tick(6)
    tick(7)
    tick(8)
    tick(9)
    tick()
    tick()

    for copy in copies[settled:]:
        copy.wait_send()


def shards(tokens, expert_ids, gate_weights, cotangent, w_gate, w_up, w_down):
    tok_rows, width = tokens.shape
    unit = w_gate.shape[1]
    seg = NZ * CAP
    slots = NX * seg
    hidden = NY * 2 * unit
    units = width // COLS
    n_copies = 27 + 8 * len(PARTS_A) + 21 + 6 + (len(PARTS_A) + len(PARTS_B)) * (3 + 7)
    hbm = pl.BlockSpec(memory_space=pl.ANY)
    vmem = pl.BlockSpec(memory_space=pltpu.VMEM)
    result = jax.ShapeDtypeStruct((tok_rows, width), BF)
    return pl.pallas_call(
        kernel,
        out_shape=(result, result),
        in_specs=[hbm] * 7,
        out_specs=(vmem, vmem),
        scratch_shapes=[
            pltpu.VMEM((3, hidden, width), BF),
            pltpu.VMEM((2, NZ * tok_rows, width), BF),
            pltpu.VMEM((NZ, 16, NZ * tok_rows), F32),
            pltpu.VMEM((8, tok_rows), jnp.int32),
            pltpu.VMEM((8, tok_rows), F32),
            pltpu.VMEM((slots, NZ * tok_rows), BF),
            pltpu.VMEM((2, NZ * tok_rows, slots), BF),
            pltpu.VMEM((2, NX - 1, seg, width), BF),
            pltpu.VMEM((2, slots, width), BF),
            pltpu.VMEM((slots, hidden), BF),
            pltpu.VMEM((2, slots, hidden), F32),
            pltpu.VMEM((slots, hidden), F32),
            pltpu.VMEM((2, slots, hidden), BF),
            pltpu.VMEM((2, NX - 1, units, seg, COLS), BF),
            pltpu.VMEM((2, units, slots, COLS), BF),
            pltpu.VMEM((2, units, NZ * tok_rows, COLS), F32),
            pltpu.VMEM((2, 2, 4, units, tok_rows, COLS), BF),
            pltpu.VMEM((2, 2, 4, units, tok_rows, COLS), BF),
            pltpu.VMEM((NZ - 1, units, tok_rows, COLS), BF),
            pltpu.VMEM((NZ - 1, units, tok_rows, COLS), BF),
            pltpu.SemaphoreType.DMA((n_copies,)),
            pltpu.SemaphoreType.DMA((n_copies,)),
            pltpu.SemaphoreType.DMA((7,)),
        ],
        compiler_params=pltpu.CompilerParams(
            collective_id=0, has_side_effects=True, vmem_limit_bytes=60 * 1024 * 1024
        ),
    )(tokens, cotangent, expert_ids.T, gate_weights.T, w_gate[0], w_up[0], w_down[0])


def solution(mesh):
    both = P(("dp", "expert"), None)
    weights = P("expert", "dp", None)
    return jax.shard_map(
        shards,
        mesh=mesh,
        in_specs=(both, both, both, both, weights, weights, weights),
        out_specs=(both, both),
        check_vma=False,
    )
```

```python
import functools

import jax
import jax.numpy as jnp
from jax import lax
from jax.experimental import pallas as pl
from jax.experimental.pallas import tpu as pltpu
from jax.sharding import PartitionSpec as P

MESH = pl.DeviceIdType.MESH
NX, NY, NZ = 4, 4, 8
CAP = 12
COLS = 256
PARTS_A = (1, 2, 2, 2, 1)
PARTS_B = (2, 2, 2, 1, 1)
RINGED = 3
NT = (((1,), (1,)), ((), ()))
BF = jnp.bfloat16
F32 = jnp.float32


def mm(a, b):
    return jnp.dot(a, b, preferred_element_type=F32)


def mm_nt(a, b):
    return lax.dot_general(a, b, NT, preferred_element_type=F32)


def kernel(
    tok_ref, cot_ref, ids_ref, gate_ref, wg_ref, wu_ref, wd_ref, out_a, out_b,
    w, t, meta, ids_in, gates_in, sel, comb, xs, rows, hid, fac, back, grads, ys, yr, part, rsend, rrecv, dsend, drecv,
    ssem, rsem, lsem,
):
    dp, ex = lax.axis_index("dp"), lax.axis_index("expert")
    y, c = dp // 2, lax.rem(dp, 2)
    x, z = ex // NZ, lax.rem(ex, NZ)
    tok_rows, width = tok_ref.shape
    unit = wg_ref.shape[0]
    half = unit // 2
    seg = NZ * CAP
    hidden = 2 * NY * unit

    def at_y(step):
        return {"dp": lax.rem(y + step + NY, NY) * 2 + c, "expert": ex}

    def at_x(step):
        return {"dp": dp, "expert": lax.rem(x + step, NX) * NZ + z}

    def at_z(step):
        return {"dp": dp, "expert": x * NZ + lax.rem(z + step + NZ, NZ)}

    other = {"dp": y * 2 + 1 - c, "expert": ex}
    y_up, y_down = at_y(1), at_y(-1)
    z_dev = {1: at_z(1), -1: at_z(-1)}
    z_peers = [None] + [at_z(s) for s in range(1, NZ)]
    x_peers = [None] + [at_x(d) for d in range(1, NX)]

    barrier = pltpu.get_barrier_semaphore()
    greeted = [other, y_up, y_down] + z_peers[1:] + x_peers[1:]
    for dev in greeted:
        pl.semaphore_signal(barrier, inc=1, device_id=dev, device_id_type=MESH)

    local = []

    def local_copy(src, dst):
        copy = pltpu.make_async_copy(src, dst, lsem.at[len(local)])
        copy.start()
        local.append(copy)

    local_copy(ids_ref, ids_in)
    local_copy(gate_ref, gates_in)
    lanes = NZ * tok_rows
    token_lane = lax.broadcasted_iota(jnp.int32, (tok_rows, lanes), 0) + z * tok_rows
    spread = token_lane == lax.broadcasted_iota(jnp.int32, (tok_rows, lanes), 1)
    spread = jnp.where(spread, 1.0, 0.0).astype(BF)
    local[0].wait()
    local[1].wait()
    meta[z, 0:8] = mm((ids_in[...].astype(F32) + 1.0).astype(BF), spread)
    rest = gates_in[...]
    spread_gates = jnp.zeros((8, lanes), F32)
    for _ in range(3):
        piece = rest.astype(BF)
        spread_gates = spread_gates + mm(piece, spread)
        rest = rest - piece.astype(F32)
    meta[z, 8:16] = spread_gates
    pl.semaphore_wait(barrier, len(greeted))

    copies = []

    def send(src, dst, dev):
        i = len(copies)
        copy = pltpu.make_async_remote_copy(
            src_ref=src, dst_ref=dst, send_sem=ssem.at[i], recv_sem=rsem.at[i],
            device_id=dev, device_id_type=MESH,
        )
        copies.append(copy)
        copy.start()
        return copy

    def zrows(step):
        return pl.ds(pl.multiple_of(lax.rem(z + step + NZ, NZ) * tok_rows, tok_rows), tok_rows)

    own = [tok_ref, cot_ref, meta.at[z]]
    hops = {(0, 1): 4, (0, -1): 3, (1, 1): 3, (1, -1): 4, (2, 1): 4, (2, -1): 3}
    ring = {}

    def zplace(a, step):
        if a == 2:
            return meta.at[lax.rem(z + step + NZ, NZ)]
        return t.at[a, zrows(step)]

    def ring_start(a):
        for sign in (1, -1):
            ring[a, sign] = send(own[a], zplace(a, 0), z_dev[sign])

    def ring_step(a, step):
        for sign in (1, -1):
            if step <= hops[a, sign]:
                ring[a, sign].wait_recv()
                if step < hops[a, sign]:
                    place = zplace(a, -sign * step)
                    ring[a, sign] = send(place, place, z_dev[sign])

    mats = [wg_ref, wu_ref, wd_ref]

    def wrows(place, side, h=None):
        if h is None:
            return pl.ds((place * 2 + side) * unit, unit)
        return pl.ds((place * 2 + side) * unit + h * half, half)

    wcopy, wfwd = {}, {}
    dcols = [pl.ds(sum(PARTS_A[:j]) * COLS, PARTS_A[j] * COLS) for j in range(len(PARTS_A))]

    def issue(k):
        if k < 4:
            m, h = k // 2, k % 2
            g = 1 - h
            wcopy[m, 2, h] = send(mats[m].at[pl.ds(h * half, half)], w.at[m, wrows(2, 0, h)], y_up)
            wcopy[m, 1, g] = send(mats[m].at[pl.ds(g * half, half)], w.at[m, wrows(1, 0, g)], y_down)
        elif k < 6:
            m = k - 4
            wcopy[m, 3, 0] = send(w.at[m, wrows(2, 0, 0)], w.at[m, wrows(3, 0, 0)], y_up)
            wcopy[m, 3, 1] = send(w.at[m, wrows(1, 0, 1)], w.at[m, wrows(3, 0, 1)], y_down)
        elif k < 6 + len(PARTS_A):
            j = k - 6
            src = wd_ref.at[:, dcols[j]]
            wcopy[2, 2, j] = send(src, w.at[2, wrows(2, 0), dcols[j]], y_up)
            wcopy[2, 1, j] = send(src, w.at[2, wrows(1, 0), dcols[j]], y_down)

    def hand_over(m, p, h):
        wcopy[m, p, h].wait_recv()
        ref = w.at[m, wrows(p, 0, h)]
        wfwd[m, p, h] = send(ref, w.at[m, wrows(p, 1, h)], other)

    def event(k):
        if k < 4:
            m, h = k // 2, k % 2
            hand_over(m, 2, h)
            hand_over(m, 1, 1 - h)
        else:
            for h in (0, 1):
                hand_over(k - 4, 3, h)

    def event_down(j):
        for p, h, dev in ((2, 0, y_up), (1, 1, y_down)):
            wcopy[2, p, j].wait_recv()
            wcopy[2, 3, j, h] = send(
                w.at[2, wrows(p, 0, h), dcols[j]], w.at[2, wrows(3, 0, h), dcols[j]], dev
            )
        issue(8 + j)
        for p in (2, 1):
            wfwd[2, p, j] = send(w.at[2, wrows(p, 0), dcols[j]], w.at[2, wrows(p, 1), dcols[j]], other)

    def event_last(j):
        for h in (0, 1):
            wcopy[2, 3, j, h].wait_recv()
            wfwd[2, 3, j, h] = send(
                w.at[2, wrows(3, 0, h), dcols[j]], w.at[2, wrows(3, 1, h), dcols[j]], other
            )

    ring_start(2)
    ring_start(0)
    for k in range(4):
        issue(k)
    for a in (0, 1):
        local_copy(own[a], zplace(a, 0))
    for m in range(3):
        local_copy(mats[m], w.at[m, wrows(0, 0)])
        wfwd[m, 0] = send(mats[m], w.at[m, wrows(0, 1)], other)

    ring_step(2, 1)
    ring_step(0, 1)
    ring_start(1)
    ring_step(2, 2)
    ring_step(0, 2)
    ring_step(1, 1)
    ring_step(2, 3)
    ring_step(0, 3)
    ring_step(1, 2)
    ring_step(2, 4)
    ring_step(0, 4)
    for copy in local[2:4]:
        copy.wait()

    table = meta[0]
    for i in range(1, NZ):
        table = table + meta[i]
    count = NZ * tok_rows
    lane_of = lax.broadcasted_iota(jnp.int32, (count, count), 1)
    line_of = lax.broadcasted_iota(jnp.int32, (count, count), 0)
    before = ((lane_of >> 5) == (line_of >> 5)) & (line_of < lane_of)
    before = jnp.where(before, 1.0, 0.0).astype(BF)
    line8 = lax.broadcasted_iota(jnp.int32, (8, count), 0)
    base8 = ((lax.broadcasted_iota(jnp.int32, (8, count), 1) >> 5) * CAP).astype(F32)
    taken = jnp.zeros((8, count), F32)
    gates = []
    for d in range(NX):
        number = (lax.rem(x + d, NX) * NZ + z + 1).astype(F32)
        hit = jnp.where(table[0:8] == number, 1.0, 0.0)
        taken = jnp.where(line8 == d, jnp.sum(hit, axis=0, keepdims=True), taken)
        gates.append(jnp.sum(hit * table[8:16], axis=0, keepdims=True))
    place = base8 + mm(taken.astype(BF), before)
    place = jnp.where(taken > 0.5, place, -1.0)
    line_seg = lax.broadcasted_iota(jnp.int32, (seg, count), 0).astype(F32)
    weighted = []
    for d in range(NX):
        one = jnp.where(line_seg == place[d : d + 1], 1.0, 0.0)
        sel[pl.ds(d * seg, seg), :] = one.astype(BF)
        weighted.append(one * gates[d])

    xcopy = {}

    def pick(a):
        @pl.loop(0, 4)
        def _(i):
            cols = pl.ds(pl.multiple_of(i * (width // 4), width // 4), width // 4)
            got = mm(sel[...], t[a, :, cols]).astype(BF)
            rows[a, pl.ds(0, seg), cols] = got[0:seg]
            for d in range(1, NX):
                xs[a, d - 1, :, cols] = got[d * seg : (d + 1) * seg]

    def send_rows(a):
        for d in (2, 1, 3):
            xcopy[a, d] = send(xs.at[a, d - 1], rows.at[a, pl.ds((NX - d) * seg, seg)], x_peers[d])

    pick(0)
    send_rows(0)
    event(0)
    issue(4)
    event(1)
    ring_step(1, 3)
    event(2)
    for k in range(5, 8):
        issue(k)
    weighted = jnp.concatenate(weighted, axis=0).T
    high = weighted.astype(BF)
    comb[0] = high
    comb[1] = (weighted - high.astype(F32)).astype(BF)
    ring_step(1, 4)
    pick(1)
    send_rows(1)
    event(3)
    event(4)
    for d in range(1, NX):
        xcopy[0, d].wait_recv()

    def first(row0, tiles, tile):
        @pl.loop(0, tiles)
        def _(i):
            span = pl.ds(pl.multiple_of(row0 + i * tile, 128), tile)
            gate = mm_nt(rows[0], w[0, span, :])
            up = mm_nt(rows[0], w[1, span, :])
            sig = jax.nn.sigmoid(gate)
            silu = gate * sig
            hid[:, span] = (silu * up).astype(BF)
            fac[0, :, span] = up * sig * (1.0 + gate * (1.0 - sig))
            fac[1, :, span] = silu

    pair = 2 * unit
    for m in (0, 1):
        local[4 + m].wait()
        wfwd[m, 0].wait_recv()
    first(0, 1, pair)
    for m in (0, 1):
        for p in (1, 2):
            for h in (0, 1):
                wfwd[m, p, h].wait_recv()
    first(pair, 3, 256)
    event(5)
    for m in (0, 1):
        for h in (0, 1):
            wfwd[m, 3, h].wait_recv()
    first(3 * pair, 1, pair)

    chunks = []
    for a, parts in enumerate((PARTS_A, PARTS_B)):
        for i, n in enumerate(parts):
            chunks.append((a, sum(parts[:i]), n, a == 0 or i < RINGED))
    ycopy, chain = {}, {}
    outs = [out_a, out_b]

    def send_back(q, done):
        a, u, n, _ = chunks[q]
        for d in (2, 1, 3):
            for i in range(n):
                ys[a, d - 1, u + i] = done[d * seg : (d + 1) * seg, i * COLS : (i + 1) * COLS]
            ycopy[q, d] = send(
                ys.at[a, d - 1, pl.ds(u, n)],
                yr.at[a, pl.ds(u, n), pl.ds((NX - d) * seg, seg)],
                x_peers[d],
            )
        for i in range(n):
            yr[a, u + i, pl.ds(0, seg), :] = done[0:seg, i * COLS : (i + 1) * COLS]

    def gather_back(q):
        a, u, n, _ = chunks[q]
        for d in range(1, NX):
            ycopy[q, d].wait_recv()
        for i in range(u, u + n):
            part[a, i] = mm(comb[0], yr[a, i]) + mm(comb[1], yr[a, i])

    def direct_sum(q, step):
        a, u, n, _ = chunks[q]
        if step == 1:
            for s in (4, 3, 5, 2, 6, 1, 7):
                dsend[s - 1, pl.ds(u, n)] = part[a, pl.ds(u, n), zrows(s), :].astype(BF)
                chain[q, s] = send(
                    dsend.at[s - 1, pl.ds(u, n)], drecv.at[s - 1, pl.ds(u, n)], z_peers[s]
                )
            return
        for s in range(1, NZ):
            chain[q, s].wait_recv()
        for i in range(u, u + n):
            total = part[a, i, zrows(0), :]
            for s in range(1, NZ):
                total = total + drecv[s - 1, i].astype(F32)
            outs[a][:, pl.ds(i * COLS, COLS)] = total.astype(BF)

    def ring_sum(q, step):
        a, u, n, _ = chunks[q]
        if step == 5:
            for k in (0, 1):
                chain[q, k].wait_recv()
            for i in range(u, u + n):
                total = part[a, i, zrows(0), :]
                for k, sign in enumerate((1, -1)):
                    total = total + rrecv[a, k, hops[a, sign] - 1, i].astype(F32)
                outs[a][:, pl.ds(i * COLS, COLS)] = total.astype(BF)
            return
        for k, sign in enumerate((1, -1)):
            far = hops[a, sign]
            if step > far:
                continue
            some = pl.ds(u, n)
            term = part[a, some, zrows(sign * (far - step + 1)), :]
            if step > 1:
                chain[q, k].wait_recv()
                term = term + rrecv[a, k, step - 2, some].astype(F32)
            rsend[a, k, step - 1, some] = term.astype(BF)
            chain[q, k] = send(
                rsend.at[a, k, step - 1, some], rrecv.at[a, k, step - 1, some], z_dev[sign]
            )

    begun = []

    def tick(*starting):
        for q, age in begun:
            if chunks[q][3] and age <= 5:
                ring_sum(q, age)
        for q, age in begun:
            if not chunks[q][3] and age == 3:
                direct_sum(q, 2)
        begun[:] = [(q, age + 1) for q, age in begun]
        for q in starting:
            gather_back(q)
            (ring_sum if chunks[q][3] else direct_sum)(q, 1)
            begun.append((q, 2))

    def layer_chunk(j):
        if j == 0:
            local[6].wait()
            wfwd[2, 0].wait_recv()
        for p in (1, 2):
            wfwd[2, p, j].wait_recv()
        for h in (0, 1):
            wfwd[2, 3, j, h].wait_recv()
        send_back(j, mm(hid[...], w[2, :, dcols[j]]).astype(BF))

    def back_chunk(j):
        @pl.loop(0, hidden // 256)
        def _(i):
            span = pl.ds(pl.multiple_of(i * 256, 256), 256)
            term = mm_nt(rows[1, :, dcols[j]], w[2, span, dcols[j]])
            if j > 0:
                term = term + back[:, span]
            if j + 1 < len(PARTS_A):
                back[:, span] = term
            else:
                grads[0, :, span] = (term * fac[0, :, span]).astype(BF)
                grads[1, :, span] = (term * fac[1, :, span]).astype(BF)

    def grad_chunk(q):
        _, u, n, _ = chunks[q]
        cols = pl.ds(u * COLS, n * COLS)
        done = mm(grads[0], w[0, :, cols]) + mm(grads[1], w[1, :, cols])
        send_back(q, done.astype(BF))

    event_down(0)
    event_down(1)
    event_last(0)
    layer_chunk(0)
    for d in range(1, NX):
        xcopy[1, d].wait_recv()
    back_chunk(0)
    event_down(2)
    event_last(1)
    layer_chunk(1)
    back_chunk(1)
    tick(0)
    event_down(3)
    event_last(2)
    layer_chunk(2)
    event_down(4)
    back_chunk(2)
    tick(1)
    event_last(3)
    layer_chunk(3)
    event_last(4)
    back_chunk(3)
    layer_chunk(4)
    settled = len(copies)
    back_chunk(4)
    grad_chunk(5)
    grad_chunk(6)
    grad_chunk(7)
    tick(2, 3, 4)
    grad_chunk(8)
    grad_chunk(9)
    tick(5)
    for copy in copies[:settled]:
        copy.wait_send()
    tick(6)
    tick(7)
    tick(8)
    later = len(copies)
    for copy in copies[settled:later]:
        copy.wait_send()
    tick(9)
    tick()
    tick()

    for copy in copies[later:]:
        copy.wait_send()


def shards(tokens, expert_ids, gate_weights, cotangent, w_gate, w_up, w_down):
    tok_rows, width = tokens.shape
    unit = w_gate.shape[1]
    seg = NZ * CAP
    slots = NX * seg
    hidden = NY * 2 * unit
    units = width // COLS
    n_copies = 27 + 8 * len(PARTS_A) + 21 + 6 + (len(PARTS_A) + len(PARTS_B)) * (3 + 7)
    hbm = pl.BlockSpec(memory_space=pl.ANY)
    vmem = pl.BlockSpec(memory_space=pltpu.VMEM)
    result = pltpu.VMEM((tok_rows, width), BF)
    return pl.pallas_call(
        kernel,
        out_shape=(result, result),
        in_specs=[hbm] * 7,
        out_specs=(vmem, vmem),
        scratch_shapes=[
            pltpu.VMEM((3, hidden, width), BF),
            pltpu.VMEM((2, NZ * tok_rows, width), BF),
            pltpu.VMEM((NZ, 16, NZ * tok_rows), F32),
            pltpu.VMEM((8, tok_rows), jnp.int32),
            pltpu.VMEM((8, tok_rows), F32),
            pltpu.VMEM((slots, NZ * tok_rows), BF),
            pltpu.VMEM((2, NZ * tok_rows, slots), BF),
            pltpu.VMEM((2, NX - 1, seg, width), BF),
            pltpu.VMEM((2, slots, width), BF),
            pltpu.VMEM((slots, hidden), BF),
            pltpu.VMEM((2, slots, hidden), F32),
            pltpu.VMEM((slots, hidden), F32),
            pltpu.VMEM((2, slots, hidden), BF),
            pltpu.VMEM((2, NX - 1, units, seg, COLS), BF),
            pltpu.VMEM((2, units, slots, COLS), BF),
            pltpu.VMEM((2, units, NZ * tok_rows, COLS), F32),
            pltpu.VMEM((2, 2, 4, units, tok_rows, COLS), BF),
            pltpu.VMEM((2, 2, 4, units, tok_rows, COLS), BF),
            pltpu.VMEM((NZ - 1, units, tok_rows, COLS), BF),
            pltpu.VMEM((NZ - 1, units, tok_rows, COLS), BF),
            pltpu.SemaphoreType.DMA((n_copies,)),
            pltpu.SemaphoreType.DMA((n_copies,)),
            pltpu.SemaphoreType.DMA((7,)),
        ],
        compiler_params=pltpu.CompilerParams(
            collective_id=0, has_side_effects=True, vmem_limit_bytes=60 * 1024 * 1024
        ),
    )(tokens, cotangent, expert_ids.T, gate_weights.T, w_gate[0], w_up[0], w_down[0])


def solution(mesh):
    both = P(("dp", "expert"), None)
    weights = P("expert", "dp", None)
    return jax.shard_map(
        shards,
        mesh=mesh,
        in_specs=(both, both, both, both, weights, weights, weights),
        out_specs=(both, both),
        check_vma=False,
    )
```

```python
import functools

import jax
import jax.numpy as jnp
from jax import lax
from jax.experimental import pallas as pl
from jax.experimental.pallas import tpu as pltpu
from jax.sharding import PartitionSpec as P

MESH = pl.DeviceIdType.MESH
NX, NY, NZ = 4, 4, 8
CAP = 12
COLS = 256
PARTS_A = (1, 2, 2, 2, 1)
PARTS_B = (2, 2, 2, 1, 1)
RINGED = 3
NT = (((1,), (1,)), ((), ()))
BF = jnp.bfloat16
F32 = jnp.float32


def mm(a, b):
    return jnp.dot(a, b, preferred_element_type=F32)


def mm_nt(a, b):
    return lax.dot_general(a, b, NT, preferred_element_type=F32)


def kernel(
    tok_ref, cot_ref, ids_ref, gate_ref, wg_ref, wu_ref, wd_ref, out_a, out_b,
    w, t, meta, ids_in, gates_in, sel, comb, xs, rows, hid, fac, back, grads, ys, yr, part, rsend, rrecv, dsend, drecv,
    ssem, rsem, lsem,
):
    dp, ex = lax.axis_index("dp"), lax.axis_index("expert")
    y, c = dp // 2, lax.rem(dp, 2)
    x, z = ex // NZ, lax.rem(ex, NZ)
    tok_rows, width = tok_ref.shape
    unit = wg_ref.shape[0]
    half = unit // 2
    seg = NZ * CAP
    hidden = 2 * NY * unit

    def at_y(step):
        return {"dp": lax.rem(y + step + NY, NY) * 2 + c, "expert": ex}

    def at_x(step):
        return {"dp": dp, "expert": lax.rem(x + step, NX) * NZ + z}

    def at_z(step):
        return {"dp": dp, "expert": x * NZ + lax.rem(z + step + NZ, NZ)}

    other = {"dp": y * 2 + 1 - c, "expert": ex}
    y_up, y_down = at_y(1), at_y(-1)
    z_dev = {1: at_z(1), -1: at_z(-1)}
    z_peers = [None] + [at_z(s) for s in range(1, NZ)]
    x_peers = [None] + [at_x(d) for d in range(1, NX)]

    barrier = pltpu.get_barrier_semaphore()
    greeted = [other, y_up, y_down] + z_peers[1:] + x_peers[1:]
    for dev in greeted:
        pl.semaphore_signal(barrier, inc=1, device_id=dev, device_id_type=MESH)

    local = []

    def local_copy(src, dst):
        copy = pltpu.make_async_copy(src, dst, lsem.at[len(local)])
        copy.start()
        local.append(copy)

    local_copy(ids_ref, ids_in)
    local_copy(gate_ref, gates_in)
    lanes = NZ * tok_rows
    token_lane = lax.broadcasted_iota(jnp.int32, (tok_rows, lanes), 0) + z * tok_rows
    spread = token_lane == lax.broadcasted_iota(jnp.int32, (tok_rows, lanes), 1)
    spread = jnp.where(spread, 1.0, 0.0).astype(BF)
    local[0].wait()
    local[1].wait()
    meta[z, 0:8] = mm((ids_in[...].astype(F32) + 1.0).astype(BF), spread)
    rest = gates_in[...]
    spread_gates = jnp.zeros((8, lanes), F32)
    for _ in range(3):
        piece = rest.astype(BF)
        spread_gates = spread_gates + mm(piece, spread)
        rest = rest - piece.astype(F32)
    meta[z, 8:16] = spread_gates
    pl.semaphore_wait(barrier, len(greeted))

    copies = []

    def send(src, dst, dev):
        i = len(copies)
        copy = pltpu.make_async_remote_copy(
            src_ref=src, dst_ref=dst, send_sem=ssem.at[i], recv_sem=rsem.at[i],
            device_id=dev, device_id_type=MESH,
        )
        copies.append(copy)
        copy.start()
        return copy

    def zrows(step):
        return pl.ds(pl.multiple_of(lax.rem(z + step + NZ, NZ) * tok_rows, tok_rows), tok_rows)

    own = [tok_ref, cot_ref, meta.at[z]]
    hops = {(0, 1): 4, (0, -1): 3, (1, 1): 3, (1, -1): 4, (2, 1): 4, (2, -1): 3}
    ring = {}

    def zplace(a, step):
        if a == 2:
            return meta.at[lax.rem(z + step + NZ, NZ)]
        return t.at[a, zrows(step)]

    def ring_start(a):
        for sign in (1, -1):
            ring[a, sign] = send(own[a], zplace(a, 0), z_dev[sign])

    def ring_step(a, step):
        for sign in (1, -1):
            if step <= hops[a, sign]:
                ring[a, sign].wait_recv()
                if step < hops[a, sign]:
                    place = zplace(a, -sign * step)
                    ring[a, sign] = send(place, place, z_dev[sign])

    mats = [wg_ref, wu_ref, wd_ref]

    def wrows(place, side, h=None):
        if h is None:
            return pl.ds((place * 2 + side) * unit, unit)
        return pl.ds((place * 2 + side) * unit + h * half, half)

    wcopy, wfwd = {}, {}
    dcols = [pl.ds(sum(PARTS_A[:j]) * COLS, PARTS_A[j] * COLS) for j in range(len(PARTS_A))]

    def issue(k):
        if k < 4:
            m, h = k // 2, k % 2
            g = 1 - h
            wcopy[m, 2, h] = send(mats[m].at[pl.ds(h * half, half)], w.at[m, wrows(2, 0, h)], y_up)
            wcopy[m, 1, g] = send(mats[m].at[pl.ds(g * half, half)], w.at[m, wrows(1, 0, g)], y_down)
        elif k < 6:
            m = k - 4
            wcopy[m, 3, 0] = send(w.at[m, wrows(2, 0, 0)], w.at[m, wrows(3, 0, 0)], y_up)
            wcopy[m, 3, 1] = send(w.at[m, wrows(1, 0, 1)], w.at[m, wrows(3, 0, 1)], y_down)
        elif k < 6 + len(PARTS_A):
            j = k - 6
            src = wd_ref.at[:, dcols[j]]
            wcopy[2, 2, j] = send(src, w.at[2, wrows(2, 0), dcols[j]], y_up)
            wcopy[2, 1, j] = send(src, w.at[2, wrows(1, 0), dcols[j]], y_down)

    def hand_over(m, p, h):
        wcopy[m, p, h].wait_recv()
        ref = w.at[m, wrows(p, 0, h)]
        wfwd[m, p, h] = send(ref, w.at[m, wrows(p, 1, h)], other)

    def event(k):
        if k < 4:
            m, h = k // 2, k % 2
            hand_over(m, 2, h)
            hand_over(m, 1, 1 - h)
        else:
            for h in (0, 1):
                hand_over(k - 4, 3, h)

    def event_down(j):
        for p, h, dev in ((2, 0, y_up), (1, 1, y_down)):
            wcopy[2, p, j].wait_recv()
            wcopy[2, 3, j, h] = send(
                w.at[2, wrows(p, 0, h), dcols[j]], w.at[2, wrows(3, 0, h), dcols[j]], dev
            )
        issue(8 + j)
        for p in (2, 1):
            wfwd[2, p, j] = send(w.at[2, wrows(p, 0), dcols[j]], w.at[2, wrows(p, 1), dcols[j]], other)

    def event_last(j):
        for h in (0, 1):
            wcopy[2, 3, j, h].wait_recv()
            wfwd[2, 3, j, h] = send(
                w.at[2, wrows(3, 0, h), dcols[j]], w.at[2, wrows(3, 1, h), dcols[j]], other
            )

    ring_start(2)
    ring_start(0)
    for k in range(4):
        issue(k)
    for a in (0, 1):
        local_copy(own[a], zplace(a, 0))
    for m in range(3):
        local_copy(mats[m], w.at[m, wrows(0, 0)])
        wfwd[m, 0] = send(mats[m], w.at[m, wrows(0, 1)], other)

    ring_step(2, 1)
    ring_step(0, 1)
    ring_start(1)
    ring_step(2, 2)
    ring_step(0, 2)
    ring_step(1, 1)
    ring_step(2, 3)
    ring_step(0, 3)
    ring_step(1, 2)
    ring_step(2, 4)
    ring_step(0, 4)
    for copy in local[2:4]:
        copy.wait()

    table = meta[0]
    for i in range(1, NZ):
        table = table + meta[i]
    count = NZ * tok_rows
    lane_of = lax.broadcasted_iota(jnp.int32, (count, count), 1)
    line_of = lax.broadcasted_iota(jnp.int32, (count, count), 0)
    before = ((lane_of >> 5) == (line_of >> 5)) & (line_of < lane_of)
    before = jnp.where(before, 1.0, 0.0).astype(BF)
    line8 = lax.broadcasted_iota(jnp.int32, (8, count), 0)
    base8 = ((lax.broadcasted_iota(jnp.int32, (8, count), 1) >> 5) * CAP).astype(F32)
    taken = jnp.zeros((8, count), F32)
    gates = []
    for d in range(NX):
        number = (lax.rem(x + d, NX) * NZ + z + 1).astype(F32)
        hit = jnp.where(table[0:8] == number, 1.0, 0.0)
        taken = jnp.where(line8 == d, jnp.sum(hit, axis=0, keepdims=True), taken)
        gates.append(jnp.sum(hit * table[8:16], axis=0, keepdims=True))
    place = base8 + mm(taken.astype(BF), before)
    place = jnp.where(taken > 0.5, place, -1.0)
    line_seg = lax.broadcasted_iota(jnp.int32, (seg, count), 0).astype(F32)
    weighted = []
    for d in range(NX):
        one = jnp.where(line_seg == place[d : d + 1], 1.0, 0.0)
        sel[pl.ds(d * seg, seg), :] = one.astype(BF)
        weighted.append(one * gates[d])

    xcopy = {}

    def pick(a):
        @pl.loop(0, 4)
        def _(i):
            cols = pl.ds(pl.multiple_of(i * (width // 4), width // 4), width // 4)
            got = mm(sel[...], t[a, :, cols]).astype(BF)
            rows[a, pl.ds(0, seg), cols] = got[0:seg]
            for d in range(1, NX):
                xs[a, d - 1, :, cols] = got[d * seg : (d + 1) * seg]

    def send_rows(a):
        for d in (2, 1, 3):
            xcopy[a, d] = send(xs.at[a, d - 1], rows.at[a, pl.ds((NX - d) * seg, seg)], x_peers[d])

    pick(0)
    send_rows(0)
    event(0)
    issue(4)
    event(1)
    ring_step(1, 3)
    event(2)
    for k in range(5, 8):
        issue(k)
    weighted = jnp.concatenate(weighted, axis=0).T
    high = weighted.astype(BF)
    comb[0] = high
    comb[1] = (weighted - high.astype(F32)).astype(BF)
    ring_step(1, 4)
    pick(1)
    send_rows(1)
    event(3)
    event(4)
    for d in range(1, NX):
        xcopy[0, d].wait_recv()

    def first(row0, tiles, tile):
        @pl.loop(0, tiles)
        def _(i):
            span = pl.ds(pl.multiple_of(row0 + i * tile, 128), tile)
            gate = mm_nt(rows[0], w[0, span, :])
            up = mm_nt(rows[0], w[1, span, :])
            sig = jax.nn.sigmoid(gate)
            silu = gate * sig
            hid[:, span] = (silu * up).astype(BF)
            fac[0, :, span] = up * sig * (1.0 + gate * (1.0 - sig))
            fac[1, :, span] = silu

    pair = 2 * unit
    for m in (0, 1):
        local[4 + m].wait()
        wfwd[m, 0].wait_recv()
    first(0, 1, pair)
    for m in (0, 1):
        for p in (1, 2):
            for h in (0, 1):
                wfwd[m, p, h].wait_recv()
    first(pair, 3, 256)
    event(5)
    for m in (0, 1):
        for h in (0, 1):
            wfwd[m, 3, h].wait_recv()
    first(3 * pair, 1, pair)

    chunks = []
    for a, parts in enumerate((PARTS_A, PARTS_B)):
        for i, n in enumerate(parts):
            chunks.append((a, sum(parts[:i]), n, a == 0 or i < RINGED))
    ycopy, chain = {}, {}
    outs = [out_a, out_b]

    def send_back(q, done):
        a, u, n, _ = chunks[q]
        for d in (2, 1, 3):
            for i in range(n):
                ys[a, d - 1, u + i] = done[d * seg : (d + 1) * seg, i * COLS : (i + 1) * COLS]
            ycopy[q, d] = send(
                ys.at[a, d - 1, pl.ds(u, n)],
                yr.at[a, pl.ds(u, n), pl.ds((NX - d) * seg, seg)],
                x_peers[d],
            )
        for i in range(n):
            yr[a, u + i, pl.ds(0, seg), :] = done[0:seg, i * COLS : (i + 1) * COLS]

    def gather_back(q):
        a, u, n, _ = chunks[q]
        for d in range(1, NX):
            ycopy[q, d].wait_recv()
        for i in range(u, u + n):
            part[a, i] = mm(comb[0], yr[a, i]) + mm(comb[1], yr[a, i])

    def direct_sum(q, step):
        a, u, n, _ = chunks[q]
        if step == 1:
            for s in (4, 3, 5, 2, 6, 1, 7):
                dsend[s - 1, pl.ds(u, n)] = part[a, pl.ds(u, n), zrows(s), :].astype(BF)
                chain[q, s] = send(
                    dsend.at[s - 1, pl.ds(u, n)], drecv.at[s - 1, pl.ds(u, n)], z_peers[s]
                )
            return
        for s in range(1, NZ):
            chain[q, s].wait_recv()
        for i in range(u, u + n):
            total = part[a, i, zrows(0), :]
            for s in range(1, NZ):
                total = total + drecv[s - 1, i].astype(F32)
            outs[a][:, pl.ds(i * COLS, COLS)] = total.astype(BF)

    def ring_sum(q, step):
        a, u, n, _ = chunks[q]
        if step == 5:
            for k in (0, 1):
                chain[q, k].wait_recv()
            for i in range(u, u + n):
                total = part[a, i, zrows(0), :]
                for k, sign in enumerate((1, -1)):
                    total = total + rrecv[a, k, hops[a, sign] - 1, i].astype(F32)
                outs[a][:, pl.ds(i * COLS, COLS)] = total.astype(BF)
            return
        for k, sign in enumerate((1, -1)):
            far = hops[a, sign]
            if step > far:
                continue
            some = pl.ds(u, n)
            term = part[a, some, zrows(sign * (far - step + 1)), :]
            if step > 1:
                chain[q, k].wait_recv()
                term = term + rrecv[a, k, step - 2, some].astype(F32)
            rsend[a, k, step - 1, some] = term.astype(BF)
            chain[q, k] = send(
                rsend.at[a, k, step - 1, some], rrecv.at[a, k, step - 1, some], z_dev[sign]
            )

    begun = []

    def tick(*starting):
        for q, age in begun:
            if chunks[q][3] and age <= 5:
                ring_sum(q, age)
        for q, age in begun:
            if not chunks[q][3] and age == 3:
                direct_sum(q, 2)
        begun[:] = [(q, age + 1) for q, age in begun]
        for q in starting:
            gather_back(q)
            (ring_sum if chunks[q][3] else direct_sum)(q, 1)
            begun.append((q, 2))

    def layer_chunk(j):
        if j == 0:
            local[6].wait()
            wfwd[2, 0].wait_recv()
        for p in (1, 2):
            wfwd[2, p, j].wait_recv()
        for h in (0, 1):
            wfwd[2, 3, j, h].wait_recv()
        send_back(j, mm(hid[...], w[2, :, dcols[j]]).astype(BF))

    def back_chunk(j):
        @pl.loop(0, hidden // 256)
        def _(i):
            span = pl.ds(pl.multiple_of(i * 256, 256), 256)
            term = mm_nt(rows[1, :, dcols[j]], w[2, span, dcols[j]])
            if j > 0:
                term = term + back[:, span]
            if j + 1 < len(PARTS_A):
                back[:, span] = term
            else:
                grads[0, :, span] = (term * fac[0, :, span]).astype(BF)
                grads[1, :, span] = (term * fac[1, :, span]).astype(BF)

    def grad_chunk(q):
        _, u, n, _ = chunks[q]
        cols = pl.ds(u * COLS, n * COLS)
        done = mm(grads[0], w[0, :, cols]) + mm(grads[1], w[1, :, cols])
        send_back(q, done.astype(BF))

    early = len(copies)
    event_down(0)
    event_down(1)
    event_last(0)
    for copy in copies[:early]:
        copy.wait_send()
    layer_chunk(0)
    for d in range(1, NX):
        xcopy[1, d].wait_recv()
    back_chunk(0)
    event_down(2)
    event_last(1)
    layer_chunk(1)
    back_chunk(1)
    tick(0)
    event_down(3)
    event_last(2)
    layer_chunk(2)
    event_down(4)
    back_chunk(2)
    tick(1)
    event_last(3)
    layer_chunk(3)
    event_last(4)
    back_chunk(3)
    layer_chunk(4)
    settled = len(copies)
    back_chunk(4)
    grad_chunk(5)
    grad_chunk(6)
    grad_chunk(7)
    grad_chunk(8)
    grad_chunk(9)
    tick(2, 3, 4, 5)
    for copy in copies[early:settled]:
        copy.wait_send()
    tick(6)
    tick(7)
    tick(8)
    later = len(copies)
    for copy in copies[settled:later]:
        copy.wait_send()
    tick(9)
    tick()
    tick()

    for copy in copies[later:]:
        copy.wait_send()


def shards(tokens, expert_ids, gate_weights, cotangent, w_gate, w_up, w_down):
    tok_rows, width = tokens.shape
    unit = w_gate.shape[1]
    seg = NZ * CAP
    slots = NX * seg
    hidden = NY * 2 * unit
    units = width // COLS
    n_copies = 27 + 8 * len(PARTS_A) + 21 + 6 + (len(PARTS_A) + len(PARTS_B)) * (3 + 7)
    hbm = pl.BlockSpec(memory_space=pl.ANY)
    vmem = pl.BlockSpec(memory_space=pltpu.VMEM)
    result = pltpu.VMEM((tok_rows, width), BF)
    return pl.pallas_call(
        kernel,
        out_shape=(result, result),
        in_specs=[hbm] * 7,
        out_specs=(vmem, vmem),
        scratch_shapes=[
            pltpu.VMEM((3, hidden, width), BF),
            pltpu.VMEM((2, NZ * tok_rows, width), BF),
            pltpu.VMEM((NZ, 16, NZ * tok_rows), F32),
            pltpu.VMEM((8, tok_rows), jnp.int32),
            pltpu.VMEM((8, tok_rows), F32),
            pltpu.VMEM((slots, NZ * tok_rows), BF),
            pltpu.VMEM((2, NZ * tok_rows, slots), BF),
            pltpu.VMEM((2, NX - 1, seg, width), BF),
            pltpu.VMEM((2, slots, width), BF),
            pltpu.VMEM((slots, hidden), BF),
            pltpu.VMEM((2, slots, hidden), F32),
            pltpu.VMEM((slots, hidden), F32),
            pltpu.VMEM((2, slots, hidden), BF),
            pltpu.VMEM((2, NX - 1, units, seg, COLS), BF),
            pltpu.VMEM((2, units, slots, COLS), BF),
            pltpu.VMEM((2, units, NZ * tok_rows, COLS), F32),
            pltpu.VMEM((2, 2, 4, units, tok_rows, COLS), BF),
            pltpu.VMEM((2, 2, 4, units, tok_rows, COLS), BF),
            pltpu.VMEM((NZ - 1, units, tok_rows, COLS), BF),
            pltpu.VMEM((NZ - 1, units, tok_rows, COLS), BF),
            pltpu.SemaphoreType.DMA((n_copies,)),
            pltpu.SemaphoreType.DMA((n_copies,)),
            pltpu.SemaphoreType.DMA((7,)),
        ],
        compiler_params=pltpu.CompilerParams(
            collective_id=0, has_side_effects=True, vmem_limit_bytes=60 * 1024 * 1024
        ),
    )(tokens, cotangent, expert_ids.T, gate_weights.T, w_gate[0], w_up[0], w_down[0])


def solution(mesh):
    both = P(("dp", "expert"), None)
    weights = P("expert", "dp", None)
    return jax.shard_map(
        shards,
        mesh=mesh,
        in_specs=(both, both, both, both, weights, weights, weights),
        out_specs=(both, both),
        check_vma=False,
    )
```
